512 devices in a mesh: vox: 32 (over z, y_lo), tm: 16 (over y_hi, x, core).
Axes of the slice: x: 4, y: 4 (y_hi: 2, y_lo: 2; y = y_hi * 2 + y_lo), z: 16, core: 2. Of those that a mesh axis runs over, the one named last changes fastest.
Arguments:
- frames_data: bfloat16 [2048, 131072], P('tm', 'vox'), may hold values from -96 to 96
- footprints: bfloat16 [131072, 384], P('vox'), may hold values from 0 to 1, as said below
- traces: bfloat16 [2048, 4096], P('tm', 'vox'), may hold values from 0 to 2
- counts: int32 [32], replicated, may hold values from 1 to 128, 2048 in all
Outputs:
- new_traces: bfloat16 [2048, 4096], P('tm', 'vox')
- products: float32 [131072, 384], P(('vox', 'tm'))
- gram: float32 [12288, 384], P('vox')
The draws below stay inside these ranges and needn't reach their ends.
Inputs may be any that keep to these rules, and one draw needn't show every extreme that they name: `footprints`: footprint entries are zero or positive. counts of live slots per tile; the largest equals 128.
All inputs are finite; a program needn't handle non-finite values.
Results may differ from the reference program's by a relative error of at most 0.0069.
Values may be sent and summed in bfloat16 or wider, within the bound.
A program may use at most 64 MiB of HBM per device.

```python
import math
import jax
import jax.numpy as jnp
import numpy as np

VT = 4096
KT = 128
ITERS = 4
TILES = 32
VOXELS = 131072
COMPS = 4096
FRAMES = 2048


def draw_footprints(key, part):
    key = jax.random.fold_in(key, 11)
    level_key, keep_key = jax.random.split(key)
    shape = (VOXELS, 3 * KT)
    level = jax.random.uniform(level_key, shape, jnp.float32, 0.25, 1.0)
    keep = jax.random.bernoulli(keep_key, 4.0 / KT, shape)
    return (level * keep.astype(jnp.float32)).astype(jnp.bfloat16)


def shard_levels(rng, dims, cuts, low, largest):
    loudness = 1.0
    for position, blocks in cuts:
        draws = jax.random.uniform(jax.random.fold_in(jax.random.fold_in(rng, 6), position), (blocks,), jnp.float32, low / len(cuts), largest / len(cuts))
        loudness = loudness * jnp.repeat(jnp.exp(draws), dims[position] // blocks).reshape((-1,) + (1,) * (len(dims) - 1 - position))
    return loudness


def length_profile(amount, total, limit, skew):
    loads = [(1 << 20) // math.isqrt(rank ** skew) + 1 for rank in range(2, amount + 1)]
    rest, given = total - limit - (amount - 1), [1] * (amount - 1)
    while rest > 0:
        candidates = [i for i in range(amount - 1) if given[i] < limit]
        pool, budget = sum([loads[i] for i in candidates]), rest
        for i in candidates:
            extra = min(limit - given[i], max(1, budget * loads[i] // pool), rest)
            given[i] = given[i] + extra
            rest = rest - extra
    return np.array([limit] + given)


def ragged(stream_key, amount, total, limit, lean):
    if amount == 2:
        one = jax.random.randint(stream_key, (), max(1, total - limit), min(limit, total - 1) + 1)
        return jnp.stack([one, total - one])
    tallies = jnp.asarray(length_profile(amount, total, limit, lean), jnp.int32)
    couples = (amount - 1) // 2
    source_of, taker = tallies[1:1 + 2 * couples:2], tallies[2:2 + 2 * couples:2]
    slack = jnp.minimum(source_of - 1, limit - taker)
    passed = jax.random.randint(jax.random.fold_in(stream_key, 1), (couples,), 0, 1 << 20) % (slack + 1)
    tallies = tallies.at[1:1 + 2 * couples:2].set(source_of - passed).at[2:2 + 2 * couples:2].set(taker + passed)
    return tallies[jax.random.permutation(jax.random.fold_in(stream_key, 2), amount)]


def scatter_about(rng, dims, deviation, most, cuts=(), kind=jnp.bfloat16):
    drawn = jax.random.normal(rng, dims, jnp.float32) * deviation
    if len(cuts) > 0:
        drawn = shard_levels(rng, dims, cuts, -0.22, 0.18) * drawn
    return jnp.clip(drawn, min=-most, max=most).astype(kind)


def setup_inputs(seed: int = 0) -> dict:
    key_of = jax.random.split(jax.random.key(seed), 5)
    frames_data = scatter_about(key_of[0], (FRAMES, VOXELS), 16.0, 96.0, ((0, 16), (1, 32)))
    footprints = draw_footprints(jax.random.fold_in(key_of[4], 71), 0)
    traces = jnp.clip(2.0 * jax.random.uniform(key_of[2], (FRAMES, COMPS), jnp.float32) ** shard_levels(key_of[2], (FRAMES, COMPS), ((0, 16), (1, 32)), -0.2, 0.2), 0.0, 2.0).astype(jnp.bfloat16)
    counts = ragged(key_of[3], TILES, TILES * KT // 2, KT, 2).astype(jnp.int32)
    return {"frames_data": frames_data, "footprints": footprints, "traces": traces, "counts": counts}


def live_columns(counts):
    tiles = counts.shape[0]
    wanted = jnp.arange(tiles, dtype=jnp.int32)[:, None] + jnp.arange(3, dtype=jnp.int32)[None, :] - 1
    inside = (wanted >= 0) & (wanted < tiles)
    picked = counts[jnp.clip(wanted, 0, tiles - 1).astype(jnp.int32)]
    number = jnp.where(inside, picked, 0)
    slots = jnp.arange(KT, dtype=jnp.int32)
    return (slots[None, None, :] < number[:, :, None]).reshape(tiles, 3 * KT)


def owner_total(parts):
    tiles, rows = parts.shape[0], parts.shape[1]
    split = parts.reshape(tiles, rows, 3, KT)
    empty = jnp.zeros((1, rows, KT), jnp.float32)
    from_left = jnp.concatenate([empty, split[:-1, :, 2]], axis=0)
    from_right = jnp.concatenate([split[1:, :, 0], empty], axis=0)
    return split[:, :, 1] + from_left + from_right


def band_of(current):
    empty = jnp.zeros_like(current[:1])
    before = jnp.concatenate([empty, current[:-1]], axis=0)
    after = jnp.concatenate([current[1:], empty], axis=0)
    stacked = jnp.stack([before, current, after], axis=2)
    return stacked.reshape(current.shape[0], current.shape[1], 3 * KT)


def reference(frames_data, footprints, traces, counts):
    live = live_columns(counts)
    blocks = footprints.reshape(TILES, VT, 3 * KT) * live[:, None, :].astype(footprints.dtype)
    own_live = live[:, KT:2 * KT].astype(jnp.float32)
    movie = frames_data.reshape(FRAMES, TILES, VT).transpose(1, 0, 2)
    current = traces.reshape(FRAMES, TILES, KT).transpose(1, 0, 2)
    current = current * own_live[:, None, :].astype(current.dtype)
    blocks_wide = blocks.astype(jnp.float32)
    support = jnp.sum(blocks_wide, axis=2).astype(jnp.bfloat16)
    reach = jnp.einsum('tv,tvk->tk', support.astype(jnp.float32), blocks_wide)
    majorant = jnp.maximum(owner_total(reach[:, None, :])[:, 0], 1.0)
    movie_wide = movie.astype(jnp.float32)
    for step in range(ITERS):
        band = band_of(current).astype(jnp.float32)
        recon = jnp.einsum('tfk,tvk->tfv', band, blocks_wide)
        resid = (movie_wide - recon).astype(jnp.bfloat16)
        parts = jnp.einsum('tfv,tvk->tfk', resid.astype(jnp.float32), blocks_wide)
        slope = owner_total(parts)
        updated = jnp.maximum(current.astype(jnp.float32) + slope / majorant[:, None, :], 0.0)
        current = (updated * own_live[:, None, :]).astype(jnp.bfloat16)
    band = band_of(current).astype(jnp.float32)
    products = jnp.einsum('tfv,tfk->tvk', movie_wide, band)
    gram = jnp.einsum('tfj,tfk->tjk', band, band)
    new_traces = current.transpose(1, 0, 2).reshape(FRAMES, COMPS)
    return new_traces, products.reshape(VOXELS, 3 * KT), gram.reshape(TILES * 3 * KT, 3 * KT)
```

```python
import functools

import jax
import jax.numpy as jnp
from jax import lax
from jax.experimental import pallas as pl
from jax.experimental.pallas import tpu as pltpu
from jax.sharding import PartitionSpec as P

ITERS = 4
CHUNK = 512
MESH = pl.DeviceIdType.MESH
F32 = jnp.float32
BF16 = jnp.bfloat16


def position():
    vox, tm = lax.axis_index("vox"), lax.axis_index("tm")
    return vox // 2, vox % 2, tm // 2, tm % 2


def turned(quad, dy, dx):
    return ((quad // 4 + dy) % 2) * 4 + (quad % 4 + dx) % 4


def exchange_kernel(
    planes,
    counts_ref, frames_ref, prints_ref, traces_ref,
    movie_ref, band_ref, edge_ref,
    prints, frames, tracebuf, gacc, facc,
    part_plane, part_edge, got_plane, got_edge,
    gram_plane, gram_edge, got_gram, mixing,
    state, final, final_edge,
    load_sem, movie_send, movie_recv, trace_send, trace_recv, part_send, part_recv,
    gram_send, gram_recv, state_send, state_recv, band_send, band_recv,
    edge_send, edge_recv, pass_send, pass_recv, own_sem,
):
    z, l, quad, core = position()
    other = 1 - l
    up, down = (z + 1) % planes, (z + planes - 1) % planes
    outward = (z + planes - 1 + 2 * l) % planes

    def device(plane, side, q, c):
        return (plane * 2 + side, q * 2 + c)

    me = device(z, l, quad, core)
    offsets = [(dy, dx) for dy in range(2) for dx in range(4)]
    barrier = pltpu.get_barrier_semaphore()
    greeted = 0
    for dy, dx in offsets:
        back = turned(quad, -dy + 2, -dx + 4)
        for dc in range(2):
            if (dy, dx, dc) != (0, 0, 0):
                pl.semaphore_signal(barrier, inc=1, device_id=device(z, l, back, (core + dc) % 2), device_id_type=MESH)
                greeted += 1
        pl.semaphore_signal(barrier, inc=1, device_id=device(z, other, back, core), device_id_type=MESH)
        greeted += 1
        inward = (z + planes + 2 * l - 1) % planes
        for side in range(2):
            pl.semaphore_signal(barrier, inc=1, device_id=device(inward, side, back, core), device_id_type=MESH)
            greeted += 1
    far = (z + planes + 1 - 2 * l) % planes
    for side in range(2):
        pl.semaphore_signal(barrier, inc=1, device_id=device(far, side, quad, core), device_id_type=MESH)
        greeted += 1

    rows = prints_ref.shape[0]
    chunks = rows // CHUNK
    plane_at = pl.multiple_of((1 - l) * 128, 128)
    edge_at = pl.multiple_of(l * 256, 128)

    def loads(k):
        at = pl.multiple_of(k * CHUNK, CHUNK)
        return (
            pltpu.make_async_copy(prints_ref.at[pl.ds(at, CHUNK), pl.ds(plane_at, 256)], prints.at[pl.ds(at, CHUNK), pl.ds(0, 256)], load_sem.at[k, 0]),
            pltpu.make_async_copy(prints_ref.at[pl.ds(at, CHUNK), pl.ds(edge_at, 128)], prints.at[pl.ds(at, CHUNK), pl.ds(256, 128)], load_sem.at[k, 1]),
            pltpu.make_async_copy(frames_ref.at[:, :, pl.ds(at, CHUNK)], frames.at[:, :, pl.ds(at, CHUNK)], load_sem.at[k, 2]),
        )

    own_trace = pltpu.make_async_copy(traces_ref, tracebuf.at[2 + l], own_sem.at[0])
    own_trace.start()
    for k in range(chunks):
        for copy in loads(k):
            copy.start()
    share = movie_ref.shape[4]
    own_movie = pltpu.make_async_copy(
        frames_ref.at[:, :, pl.ds(pl.multiple_of((quad * 2 + core) * share, share), share)],
        movie_ref.at[core, :, quad], own_sem.at[1])
    own_movie.start()

    pl.semaphore_wait(barrier, greeted)

    def trace_copy(k, plane, side, slot):
        return pltpu.make_async_remote_copy(
            traces_ref, tracebuf.at[slot], trace_send.at[k], trace_recv.at[slot],
            device_id=device(plane, side, quad, core), device_id_type=MESH)

    trace_copies = [
        trace_copy(0, z, other, 2 + l),
        trace_copy(1, up, 0, l), trace_copy(2, up, 1, l),
        trace_copy(3, down, 0, 4 + l), trace_copy(4, down, 1, 4 + l),
    ]
    for copy in trace_copies:
        copy.start()

    movie_copies = []
    for dc in range(2):
        for dy, dx in offsets:
            if (dy, dx, dc) != (0, 0, 0):
                q, c = turned(quad, dy, dx), (core + dc) % 2
                slot = (dy * 4 + dx) * 2 + dc
                movie_copies.append(pltpu.make_async_remote_copy(
                    frames_ref.at[:, :, pl.ds(pl.multiple_of((q * 2 + c) * share, share), share)],
                    movie_ref.at[core, :, quad], movie_send.at[slot], movie_recv.at[slot],
                    device_id=device(z, l, q, c), device_id_type=MESH))
    for copy in movie_copies:
        copy.start()

    def number(tile):
        inside = jnp.logical_and(tile >= 0, tile < 2 * planes)
        return jnp.where(inside, counts_ref[jnp.clip(tile, 0, 2 * planes - 1)], 0)

    numbers = [number(2 * z - 2 + s) for s in range(6)]
    edge_number = jnp.where(l == 0, numbers[1], numbers[4])

    lane = lax.broadcasted_iota(jnp.int32, (1, 128), 1)
    row = lax.broadcasted_iota(jnp.int32, (128, 1), 0)
    live_rows = jnp.concatenate(
        [(row < n).astype(F32) for n in (numbers[2], numbers[3], edge_number)], axis=0)
    live_lanes = [(lane < n).astype(F32) for n in numbers]
    own_live = jnp.concatenate([live_lanes[2], live_lanes[3]], axis=1)

    gacc[...] = jnp.zeros_like(gacc)
    facc[...] = jnp.zeros_like(facc)

    def chunk_step(k, carry):
        for copy in loads(k):
            copy.wait()
        at = pl.multiple_of(k * CHUNK, CHUNK)
        block = prints[pl.ds(at, CHUNK), :]
        turned_block = block.T
        support = jnp.sum(turned_block.astype(F32) * live_rows, axis=0, keepdims=True).astype(BF16)
        left = jnp.concatenate(
            [frames[0, :, pl.ds(at, CHUNK)], frames[1, :, pl.ds(at, CHUNK)],
             jnp.broadcast_to(support, (16, CHUNK))], axis=0)
        facc[...] += jnp.dot(left, block, preferred_element_type=F32)
        gacc[...] += jnp.dot(turned_block, block, preferred_element_type=F32)
        return carry

    lax.fori_loop(0, chunks, chunk_step, 0)

    gram = gacc[...]
    high = gram.astype(BF16)
    low = (gram - high.astype(F32)).astype(BF16)
    gram_plane[l] = high[:, :256]
    gram_edge[...] = high[:, 256:]

    own_trace.wait()

    def trace_arrival(slot):
        pltpu.make_async_remote_copy(
            traces_ref, tracebuf.at[slot], trace_send.at[0], trace_recv.at[slot],
            device_id=me, device_id_type=MESH).wait_recv()

    for slot in (0, 1, 4, 5):
        trace_arrival(slot)
    trace_arrival(2 + other)

    def trace(slot, live):
        return (tracebuf[slot].astype(F32) * live).astype(BF16)

    edge_live = jnp.where(l == 0, live_lanes[1], live_lanes[4])
    band = jnp.concatenate(
        [trace(2, live_lanes[2]), trace(3, live_lanes[3]), trace(1 + 3 * l, edge_live)], axis=1)
    reach = facc[128:136, :]
    parts = facc[0:128, :] - jnp.dot(band, high, preferred_element_type=F32) - jnp.dot(band, low, preferred_element_type=F32)
    for half in range(2):
        piece = jnp.concatenate([parts[half * 64:half * 64 + 64], reach], axis=0)
        part_plane[half] = piece[:, :256]
        part_edge[half] = piece[:, 256:]

    def to(src, dst, send, recv, plane, side):
        return pltpu.make_async_remote_copy(
            src, dst, send, recv, device_id=device(plane, side, quad, core), device_id_type=MESH)

    part_copies = [
        to(part_plane.at[other], got_plane, part_send.at[0], part_recv.at[2], z, other),
        to(part_edge.at[l], got_edge.at[other], part_send.at[1], part_recv.at[other], outward, l),
        to(part_edge.at[other], got_edge.at[other], part_send.at[2], part_recv.at[other], outward, other),
    ]
    gram_copies = [
        to(gram_plane.at[l], gram_plane.at[l], gram_send.at[0], gram_recv.at[2], z, other),
        to(gram_edge, got_gram.at[other], gram_send.at[1], gram_recv.at[other], outward, l),
        to(gram_edge, got_gram.at[other], gram_send.at[2], gram_recv.at[other], outward, other),
    ]
    for copy in part_copies + gram_copies:
        copy.start()

    mine = pl.ds(pl.multiple_of(l * 64, 64), 64)
    for s in range(6):
        value = (tracebuf[s, mine, :].astype(F32) * live_lanes[s]).astype(BF16)
        state[0, s // 2, :, (s % 2) * 128:(s % 2) * 128 + 128] = value

    to(part_plane.at[0], got_plane, part_send.at[0], part_recv.at[2], z, other).wait_recv()
    for slot in range(2):
        to(part_edge.at[0], got_edge.at[slot], part_send.at[0], part_recv.at[slot], z, other).wait_recv()
    below, above = z > 0, z < planes - 1
    total = part_plane[l] + got_plane[...] + jnp.concatenate(
        [jnp.where(below, got_edge[0], 0.0), jnp.where(above, got_edge[1], 0.0)], axis=1)
    slope = total[0:64]
    majorant = jnp.maximum(total[64:65], 1.0)

    def updated(current, slope):
        value = jnp.maximum(current.astype(F32) + slope / majorant, 0.0)
        return (value * own_live).astype(BF16)

    def send_state(step):
        copies = [
            to(state.at[step, 1], state.at[step, 0], state_send.at[step, 0], state_recv.at[step, 0], up, l),
            to(state.at[step, 1], state.at[step, 2], state_send.at[step, 1], state_recv.at[step, 1], down, l),
        ]
        for copy in copies:
            copy.start()
        return copies

    def full_state(step):
        left = jnp.where(below, state[step, 0], jnp.zeros((), BF16))
        right = jnp.where(above, state[step, 2], jnp.zeros((), BF16))
        return jnp.concatenate([left, state[step, 1], right], axis=1)

    state[1, 1] = updated(state[0, 1], slope)
    state_copies = send_state(1)

    to(gram_plane.at[0], gram_plane.at[other], gram_send.at[0], gram_recv.at[2], z, other).wait_recv()
    for slot in range(2):
        to(gram_edge, got_gram.at[slot], gram_send.at[0], gram_recv.at[slot], z, other).wait_recv()
    ga, gb = gram_plane[0].astype(F32), gram_plane[1].astype(F32)
    gc = jnp.where(below, got_gram[0].astype(F32), 0.0)
    gd = jnp.where(above, got_gram[1].astype(F32), 0.0)
    mixing[0:128, 0:128] = gc[0:128].astype(BF16)
    mixing[0:128, 128:256] = jnp.zeros((128, 128), BF16)
    mixing[128:256, 0:128] = (gc[128:256] + ga[256:384, 0:128]).astype(BF16)
    mixing[128:256, 128:256] = ga[256:384, 128:256].astype(BF16)
    mixing[256:384, 0:128] = (gc[256:384] + ga[0:128, 0:128] + gb[0:128, 0:128]).astype(BF16)
    mixing[256:384, 128:256] = (ga[0:128, 128:256] + gb[0:128, 128:256]).astype(BF16)
    mixing[384:512, 0:128] = (ga[128:256, 0:128] + gb[128:256, 0:128]).astype(BF16)
    mixing[384:512, 128:256] = (ga[128:256, 128:256] + gb[128:256, 128:256] + gd[256:384]).astype(BF16)
    mixing[512:640, 0:128] = gb[256:384, 0:128].astype(BF16)
    mixing[512:640, 128:256] = (gb[256:384, 128:256] + gd[0:128]).astype(BF16)
    mixing[640:768, 0:128] = jnp.zeros((128, 128), BF16)
    mixing[640:768, 128:256] = gd[128:256].astype(BF16)

    def mixed(step):
        return jnp.dot(full_state(step), mixing[...], preferred_element_type=F32)

    base = slope + mixed(0)
    for step in range(1, ITERS):
        for side, slot in ((0, 0), (1, 2)):
            to(state.at[step, 1], state.at[step, slot], state_send.at[step, side], state_recv.at[step, side], z, other).wait_recv()
        value = updated(state[step, 1], base - mixed(step))
        if step < ITERS - 1:
            state[step + 1, 1] = value
            state_copies += send_state(step + 1)
        else:
            final[...] = value
            final_edge[0] = value[:, :128]
            final_edge[1] = value[:, 128:]

    def band_copy(dy, dx, dl):
        slot = (dy * 4 + dx) * 2 + dl
        return pltpu.make_async_remote_copy(
            final, band_ref.at[core, l, quad], band_send.at[slot], band_recv.at[slot],
            device_id=device(z, (l + dl) % 2, turned(quad, dy, dx), core), device_id_type=MESH)

    def edge_copy(dy, dx, side):
        slot = dy * 4 + dx
        return pltpu.make_async_remote_copy(
            final_edge.at[1 - side], edge_ref.at[core, l, quad], edge_send.at[side, slot], edge_recv.at[l, slot],
            device_id=device(up if side == 0 else down, side, turned(quad, dy, dx), core), device_id_type=MESH)

    steps = [(dy, dx, dl) for dl in range(2) for dy, dx in offsets if (dy, dx, dl) != (0, 0, 0)]
    band_copies = [band_copy(*step) for step in steps]
    edge_copies = [edge_copy(dy, dx, side) for dy, dx in offsets for side in range(2)]
    own_band = pltpu.make_async_copy(final, band_ref.at[core, l, quad], own_sem.at[2])
    own_band.start()
    for copy in edge_copies + band_copies:
        copy.start()

    sibling = (z * 2 + l, quad * 2 + 1 - core)

    def pass_on(k, ref):
        return pltpu.make_async_remote_copy(
            ref.at[core], ref.at[core], pass_send.at[k], pass_recv.at[k], device_id=sibling, device_id_type=MESH)

    for copy in edge_copies:
        copy.wait_send()
    for slot in range(8):
        for side in range(2):
            pltpu.make_async_remote_copy(
                final_edge.at[0], edge_ref.at[core, side, slot], edge_send.at[0, 0], edge_recv.at[side, slot],
                device_id=me, device_id_type=MESH).wait_recv()
    pass_edge = pass_on(0, edge_ref)
    pass_edge.start()
    own_band.wait()
    for copy in band_copies:
        copy.wait()
    pass_band = pass_on(1, band_ref)
    pass_band.start()

    for k, ref in ((0, edge_ref), (1, band_ref)):
        pltpu.make_async_remote_copy(
            ref.at[1 - core], ref.at[1 - core], pass_send.at[k], pass_recv.at[k],
            device_id=me, device_id_type=MESH).wait_recv()
    pass_edge.wait_send()
    pass_band.wait_send()
    own_movie.wait()
    for copy in movie_copies:
        copy.wait()
    for copy in trace_copies + part_copies + gram_copies + state_copies:
        copy.wait_send()


def product_kernel(planes, movie_ref, band_ref, edge_ref, traces_ref, products_ref, gram_ref):
    z, l, quad, core = position()
    outside = jnp.logical_or(jnp.logical_and(l == 0, z == 0), jnp.logical_and(l == 1, z == planes - 1))
    frames = movie_ref.shape[0] * movie_ref.shape[1] * movie_ref.shape[2] * movie_ref.shape[3]
    movie = movie_ref[...].reshape(frames, movie_ref.shape[4])
    plane = band_ref[...].reshape(frames, 256)
    edge = jnp.where(outside, jnp.zeros((), BF16), edge_ref[...].reshape(frames, 128))
    whole = jnp.concatenate([plane, edge], axis=1)
    plane_at = pl.multiple_of((1 - l) * 128, 128)
    edge_at = pl.multiple_of(l * 256, 128)

    def over_frames(left):
        return lax.dot_general(left, whole, (((0,), (0,)), ((), ())), preferred_element_type=F32)

    products = over_frames(movie)
    products_ref[:, pl.ds(plane_at, 256)] = products[:, :256]
    products_ref[:, pl.ds(edge_at, 128)] = products[:, 256:]
    gram = over_frames(whole)
    gram_ref[pl.ds(plane_at, 256), pl.ds(plane_at, 256)] = gram[:256, :256]
    gram_ref[pl.ds(plane_at, 256), pl.ds(edge_at, 128)] = gram[:256, 256:]
    gram_ref[pl.ds(edge_at, 128), pl.ds(plane_at, 256)] = gram[256:, :256]
    gram_ref[pl.ds(edge_at, 128), pl.ds(edge_at, 128)] = gram[256:, 256:]
    for half in range(2):
        traces_ref[half * 64:half * 64 + 64, :] = band_ref[core, half, quad, :, pl.ds(pl.multiple_of(l * 128, 128), 128)]


def body(planes, frames_data, footprints, traces, counts):
    rows, voxels = frames_data.shape
    share = voxels // 16
    half = rows // 2
    hbm = pl.BlockSpec(memory_space=pl.ANY)
    dma = pltpu.SemaphoreType.DMA
    chunks = voxels // CHUNK
    movie, band, edge = pl.pallas_call(
        functools.partial(exchange_kernel, planes),
        name="exchange",
        out_shape=[
            jax.ShapeDtypeStruct((2, 2, 8, half, share), BF16),
            jax.ShapeDtypeStruct((2, 2, 8, half, 256), BF16),
            jax.ShapeDtypeStruct((2, 2, 8, half, 128), BF16),
        ],
        in_specs=[pl.BlockSpec(memory_space=pltpu.SMEM), hbm, hbm, hbm],
        out_specs=[hbm, hbm, hbm],
        scratch_shapes=[
            pltpu.VMEM((voxels, 384), BF16), pltpu.VMEM((2, half, voxels), BF16), pltpu.VMEM((6, rows, 128), BF16),
            pltpu.VMEM((384, 384), F32), pltpu.VMEM((rows + 16, 384), F32),
            pltpu.VMEM((2, half + 8, 256), F32), pltpu.VMEM((2, half + 8, 128), F32),
            pltpu.VMEM((half + 8, 256), F32), pltpu.VMEM((2, half + 8, 128), F32),
            pltpu.VMEM((2, 384, 256), BF16), pltpu.VMEM((384, 128), BF16), pltpu.VMEM((2, 384, 128), BF16),
            pltpu.VMEM((768, 256), BF16),
            pltpu.VMEM((ITERS, 3, half, 256), BF16), pltpu.VMEM((half, 256), BF16), pltpu.VMEM((2, half, 128), BF16),
            dma((chunks, 3)), dma((16,)), dma((16,)), dma((5,)), dma((6,)), dma((3,)), dma((3,)),
            dma((3,)), dma((3,)), dma((ITERS, 2)), dma((ITERS, 2)), dma((16,)), dma((16,)),
            dma((2, 8)), dma((2, 8)), dma((2,)), dma((2,)), dma((3,)),
        ],
        compiler_params=pltpu.CompilerParams(collective_id=0, has_side_effects=True, vmem_limit_bytes=32 << 20),
    )(counts, frames_data.reshape(2, half, voxels), footprints, traces)
    vmem = pl.BlockSpec(memory_space=pltpu.VMEM)
    return pl.pallas_call(
        functools.partial(product_kernel, planes),
        name="products",
        out_shape=[
            jax.ShapeDtypeStruct((rows, 128), BF16),
            jax.ShapeDtypeStruct((share, 384), F32),
            jax.ShapeDtypeStruct((384, 384), F32),
        ],
        in_specs=[vmem, vmem, vmem],
        out_specs=[vmem, vmem, vmem],
        compiler_params=pltpu.CompilerParams(vmem_limit_bytes=32 << 20),
    )(movie, band, edge)


def solution(mesh):
    return jax.shard_map(
        functools.partial(body, mesh.shape["vox"] // 2),
        mesh=mesh,
        in_specs=(P("tm", "vox"), P("vox", None), P("tm", "vox"), P()),
        out_specs=(P("tm", "vox"), P(("vox", "tm"), None), P("vox", None)),
        check_vma=False,
    )
```

```python
import functools

import jax
import jax.numpy as jnp
from jax import lax
from jax.experimental import pallas as pl
from jax.experimental.pallas import tpu as pltpu
from jax.sharding import PartitionSpec as P

ITERS = 4
CHUNK = 1024
MESH = pl.DeviceIdType.MESH
F32 = jnp.float32
BF16 = jnp.bfloat16


def position():
    vox, tm = lax.axis_index("vox"), lax.axis_index("tm")
    return vox // 2, vox % 2, tm // 2, tm % 2


def turned(quad, dy, dx):
    return ((quad // 4 + dy) % 2) * 4 + (quad % 4 + dx) % 4


def exchange_kernel(
    planes,
    counts_hbm, frames_ref, prints_ref, traces_ref,
    movie_ref, band_ref, edge_ref,
    counts_ref, prints, frames, tracebuf, gacc, facc,
    part_plane, part_edge, got_plane, got_edge,
    gram_plane, gram_edge, got_gram, mixing,
    state, final, final_edge,
    load_sem, movie_send, movie_recv, trace_send, trace_recv, part_send, part_recv,
    gram_send, gram_recv, state_send, state_recv, band_send, band_recv,
    edge_send, edge_recv, pass_send, pass_recv, own_sem, met,
):
    z, l, quad, core = position()
    other = 1 - l
    up, down = (z + 1) % planes, (z + planes - 1) % planes
    outward = (z + planes - 1 + 2 * l) % planes

    def device(plane, side, q, c):
        return (plane * 2 + side, q * 2 + c)

    me = device(z, l, quad, core)
    across = turned(quad, 1, 0)
    offsets = [(dy, dx) for dy in range(2) for dx in range(4)]
    ring = [(dx, dc) for dx in (1, 3, 2, 0) for dc in range(2) if (dx, dc) != (0, 0)]
    barrier = pltpu.get_barrier_semaphore()
    near = [device(z, l, turned(quad, 0, dx), (core + dc) % 2) for dx, dc in ring]
    near += [device(z, other, quad, core), device(z, l, across, core)]
    near += [device(plane, side, quad, core) for plane in (up, down) for side in range(2)]
    for target in near:
        pl.semaphore_signal(barrier, inc=1, device_id=target, device_id_type=MESH)

    rows = prints_ref.shape[0]
    chunks = rows // CHUNK
    plane_at = pl.multiple_of((1 - l) * 128, 128)
    edge_at = pl.multiple_of(l * 256, 128)

    def loads(k):
        at = pl.multiple_of(k * CHUNK, CHUNK)
        return (
            pltpu.make_async_copy(prints_ref.at[pl.ds(at, CHUNK), pl.ds(plane_at, 256)], prints.at[pl.ds(at, CHUNK), pl.ds(0, 256)], load_sem.at[k, 0]),
            pltpu.make_async_copy(prints_ref.at[pl.ds(at, CHUNK), pl.ds(edge_at, 128)], prints.at[pl.ds(at, CHUNK), pl.ds(256, 128)], load_sem.at[k, 1]),
            pltpu.make_async_copy(frames_ref.at[:, :, pl.ds(at, CHUNK)], frames.at[:, :, pl.ds(at, CHUNK)], load_sem.at[k, 2]),
        )

    own_counts = pltpu.make_async_copy(counts_hbm, counts_ref, own_sem.at[3])
    own_counts.start()
    for k in range(chunks):
        for copy in loads(k):
            copy.start()
    own_trace = pltpu.make_async_copy(traces_ref, tracebuf.at[2 + l], own_sem.at[0])
    own_trace.start()
    share = movie_ref.shape[4]
    own_movie = pltpu.make_async_copy(
        frames_ref.at[:, :, pl.ds(pl.multiple_of((quad * 2 + core) * share, share), share)],
        movie_ref.at[core, :, quad], own_sem.at[1])
    own_movie.start()
    gacc[...] = jnp.zeros_like(gacc)
    facc[...] = jnp.zeros_like(facc)
    own_counts.wait()

    def number(tile):
        inside = jnp.logical_and(tile >= 0, tile < 2 * planes)
        return jnp.where(inside, counts_ref[jnp.clip(tile, 0, 2 * planes - 1)], 0)

    numbers = [number(2 * z - 2 + s) for s in range(6)]
    edge_number = jnp.where(l == 0, numbers[1], numbers[4])
    lane = lax.broadcasted_iota(jnp.int32, (1, 128), 1)
    row = lax.broadcasted_iota(jnp.int32, (128, 1), 0)
    live_rows = jnp.concatenate(
        [(row < n).astype(F32) for n in (numbers[2], numbers[3], edge_number)], axis=0)
    live_lanes = [(lane < n).astype(F32) for n in numbers]
    own_live = jnp.concatenate([live_lanes[2], live_lanes[3]], axis=1)

    def chunk_step(k, carry):
        for copy in loads(k):
            copy.wait()
        at = pl.multiple_of(k * CHUNK, CHUNK)
        block = prints[pl.ds(at, CHUNK), :]
        flipped = block.T
        support = jnp.sum(flipped.astype(F32) * live_rows, axis=0, keepdims=True).astype(BF16)
        left = jnp.concatenate(
            [flipped[256:384], frames[0, :, pl.ds(at, CHUNK)], frames[1, :, pl.ds(at, CHUNK)],
             jnp.broadcast_to(support, (16, CHUNK))], axis=0)
        edge = jnp.dot(left, block[:, 256:384], preferred_element_type=F32)
        gacc[256:384, 256:384] += edge[0:128]
        facc[:, 256:384] += edge[128:272]
        left = jnp.concatenate([left, flipped[0:256]], axis=0)
        plane = jnp.dot(left, block[:, 0:256], preferred_element_type=F32)
        gacc[256:384, 0:256] += plane[0:128]
        facc[:, 0:256] += plane[128:272]
        gacc[0:256, 0:256] += plane[272:528]
        return carry

    chunk_step(0, 0)
    pl.semaphore_wait(barrier, len(near))
    pl.semaphore_signal(met, inc=1, device_id=device(z, l, across, core), device_id_type=MESH)

    def to(src, dst, send, recv, plane, side, q=None):
        return pltpu.make_async_remote_copy(
            src, dst, send, recv, device_id=device(plane, side, quad if q is None else q, core), device_id_type=MESH)

    trace_copies = [
        to(traces_ref, tracebuf.at[slot], trace_send.at[k], trace_recv.at[slot], plane, side)
        for k, (plane, side, slot) in enumerate(
            [(z, other, 2 + l), (up, 0, l), (up, 1, l), (down, 0, 4 + l), (down, 1, 4 + l)])
    ]
    for copy in trace_copies:
        copy.start()

    def movie_copy(dy, dx, dc):
        q, c = turned(quad, dy, dx), (core + dc) % 2
        slot = (dy * 4 + dx) * 2 + dc
        return pltpu.make_async_remote_copy(
            frames_ref.at[:, :, pl.ds(pl.multiple_of((q * 2 + c) * share, share), share)],
            movie_ref.at[core, :, quad], movie_send.at[slot], movie_recv.at[slot],
            device_id=device(z, l, q, c), device_id_type=MESH)

    movie_copies = [movie_copy(0, dx, dc) for dx, dc in ring]
    for copy in movie_copies:
        copy.start()

    lax.fori_loop(1, chunks, chunk_step, 0)

    gacc[0:256, 256:384] = gacc[256:384, 0:256].T
    gram = gacc[...]
    high = gram.astype(BF16)
    low = (gram - high.astype(F32)).astype(BF16)
    gram_plane[l] = high[:, :256]
    gram_edge[...] = high[:, 256:]

    own_trace.wait()
    for slot in (0, 1, 4, 5, 2 + other):
        to(traces_ref, tracebuf.at[slot], trace_send.at[0], trace_recv.at[slot], z, other).wait_recv()

    def trace(slot, live):
        return (tracebuf[slot].astype(F32) * live).astype(BF16)

    edge_live = jnp.where(l == 0, live_lanes[1], live_lanes[4])
    band = jnp.concatenate(
        [trace(2, live_lanes[2]), trace(3, live_lanes[3]), trace(1 + 3 * l, edge_live)], axis=1)
    reach = facc[128:136, :]
    parts = facc[0:128, :] - jnp.dot(band, high, preferred_element_type=F32) - jnp.dot(band, low, preferred_element_type=F32)
    for half in range(2):
        piece = jnp.concatenate([parts[half * 64:half * 64 + 64], reach], axis=0)
        part_plane[half] = piece[:, :256]
        part_edge[half] = piece[:, 256:]
    pl.semaphore_wait(met, 1)

    part_copies = [
        to(part_plane.at[other], got_plane, part_send.at[0], part_recv.at[2], z, other),
        to(part_edge.at[other], got_edge.at[other], part_send.at[2], part_recv.at[other], outward, other),
        to(part_edge.at[l], got_edge.at[other], part_send.at[1], part_recv.at[other], outward, l),
    ]
    own_rows = pl.ds(pl.multiple_of(core * 192, 64), 192)
    gram_copies = [
        to(gram_plane.at[l, own_rows], gram_plane.at[l, own_rows], gram_send.at[0], gram_recv.at[2], z, other, across),
        to(gram_edge.at[own_rows], got_gram.at[other, own_rows], gram_send.at[2], gram_recv.at[other], outward, other, across),
        to(gram_edge.at[own_rows], got_gram.at[other, own_rows], gram_send.at[1], gram_recv.at[other], outward, l),
    ]
    for copy in part_copies + gram_copies:
        copy.start()

    mine = pl.ds(pl.multiple_of(l * 64, 64), 64)
    for s in range(6):
        value = (tracebuf[s, mine, :].astype(F32) * live_lanes[s]).astype(BF16)
        state[0, s // 2, :, (s % 2) * 128:(s % 2) * 128 + 128] = value

    to(part_plane.at[0], got_plane, part_send.at[0], part_recv.at[2], z, other).wait_recv()
    for slot in range(2):
        to(part_edge.at[0], got_edge.at[slot], part_send.at[0], part_recv.at[slot], z, other).wait_recv()
    below, above = z > 0, z < planes - 1
    total = part_plane[l] + got_plane[...] + jnp.concatenate(
        [jnp.where(below, got_edge[0], 0.0), jnp.where(above, got_edge[1], 0.0)], axis=1)
    slope = total[0:64]
    majorant = jnp.maximum(total[64:65], 1.0)

    def updated(current, slope):
        value = jnp.maximum(current.astype(F32) + slope / majorant, 0.0)
        return (value * own_live).astype(BF16)

    def send_state(step):
        copies = [
            to(state.at[step, 1], state.at[step, 0], state_send.at[step, 0], state_recv.at[step, 0], up, l),
            to(state.at[step, 1], state.at[step, 2], state_send.at[step, 1], state_recv.at[step, 1], down, l),
        ]
        for copy in copies:
            copy.start()
        return copies

    def full_state(step):
        left = jnp.where(below, state[step, 0], jnp.zeros((), BF16))
        right = jnp.where(above, state[step, 2], jnp.zeros((), BF16))
        return jnp.concatenate([left, state[step, 1], right], axis=1)

    state[1, 1] = updated(state[0, 1], slope)
    state_copies = send_state(1)

    late_movie = [movie_copy(1, dx, dc) for dx in (0, 2, 1, 3) for dc in range(2)]
    for copy in late_movie:
        copy.start()
    movie_copies += late_movie

    sibling = (z * 2 + l, quad * 2 + 1 - core)

    def gram_pass(k, refs):
        ref = refs(own_rows)
        return pltpu.make_async_remote_copy(
            ref, ref, pass_send.at[k], pass_recv.at[k], device_id=sibling, device_id_type=MESH)

    gram_parts = [
        (2, lambda part: gram_plane.at[other, part]),
        (0, lambda part: got_gram.at[0, part]),
        (1, lambda part: got_gram.at[1, part]),
    ]
    passes = []
    for k, refs in gram_parts:
        to(refs(own_rows), refs(own_rows), gram_send.at[0], gram_recv.at[k], z, other).wait_recv()
        passes.append(gram_pass(k, refs))
        passes[-1].start()
    its_rows = pl.ds(pl.multiple_of((1 - core) * 192, 64), 192)
    for k, refs in gram_parts:
        pltpu.make_async_remote_copy(
            refs(its_rows), refs(its_rows), pass_send.at[k], pass_recv.at[k], device_id=sibling, device_id_type=MESH).wait_recv()
    ga, gb = gram_plane[0].astype(F32), gram_plane[1].astype(F32)
    gc = jnp.where(below, got_gram[0].astype(F32), 0.0)
    gd = jnp.where(above, got_gram[1].astype(F32), 0.0)
    mixing[0:128, 0:128] = gc[0:128].astype(BF16)
    mixing[0:128, 128:256] = jnp.zeros((128, 128), BF16)
    mixing[128:256, 0:128] = (gc[128:256] + ga[256:384, 0:128]).astype(BF16)
    mixing[128:256, 128:256] = ga[256:384, 128:256].astype(BF16)
    mixing[256:384, 0:128] = (gc[256:384] + ga[0:128, 0:128] + gb[0:128, 0:128]).astype(BF16)
    mixing[256:384, 128:256] = (ga[0:128, 128:256] + gb[0:128, 128:256]).astype(BF16)
    mixing[384:512, 0:128] = (ga[128:256, 0:128] + gb[128:256, 0:128]).astype(BF16)
    mixing[384:512, 128:256] = (ga[128:256, 128:256] + gb[128:256, 128:256] + gd[256:384]).astype(BF16)
    mixing[512:640, 0:128] = gb[256:384, 0:128].astype(BF16)
    mixing[512:640, 128:256] = (gb[256:384, 128:256] + gd[0:128]).astype(BF16)
    mixing[640:768, 0:128] = jnp.zeros((128, 128), BF16)
    mixing[640:768, 128:256] = gd[128:256].astype(BF16)

    def mixed(step):
        return jnp.dot(full_state(step), mixing[...], preferred_element_type=F32)

    base = slope + mixed(0)
    for step in range(1, ITERS):
        for side, slot in ((0, 0), (1, 2)):
            to(state.at[step, 1], state.at[step, slot], state_send.at[step, side], state_recv.at[step, side], z, other).wait_recv()
        value = updated(state[step, 1], base - mixed(step))
        if step < ITERS - 1:
            state[step + 1, 1] = value
            state_copies += send_state(step + 1)
        else:
            final[...] = value
            final_edge[0] = value[:, :128]
            final_edge[1] = value[:, 128:]

    def band_copy(dy, dx, dl):
        slot = (dy * 4 + dx) * 2 + dl
        return pltpu.make_async_remote_copy(
            final, band_ref.at[core, l, quad], band_send.at[slot], band_recv.at[slot],
            device_id=device(z, (l + dl) % 2, turned(quad, dy, dx), core), device_id_type=MESH)

    def edge_copy(dy, dx, side):
        slot = dy * 4 + dx
        return pltpu.make_async_remote_copy(
            final_edge.at[1 - side], edge_ref.at[core, l, quad], edge_send.at[side, slot], edge_recv.at[l, slot],
            device_id=device(up if side == 0 else down, side, turned(quad, dy, dx), core), device_id_type=MESH)

    own_band = pltpu.make_async_copy(final, band_ref.at[core, l, quad], own_sem.at[2])
    own_band.start()
    batches = [("edge", 1, 0), ("band", 1, 0), ("edge", 1, 1), ("band", 0, 1), ("edge", 0, 0), ("band", 1, 1), ("edge", 0, 1), ("band", 0, 0)]
    band_copies, edge_copies = [], []
    for kind, dy, side in batches:
        for dx in (2, 1, 3, 0):
            if kind == "edge":
                edge_copies.append(edge_copy(dy, dx, side))
                edge_copies[-1].start()
            elif (dy, dx, side) != (0, 0, 0):
                band_copies.append(band_copy(dy, dx, side))
                band_copies[-1].start()

    def row_of(kind, dy, side, c):
        yh = (quad // 4 + dy) % 2
        if kind == "edge":
            return edge_ref.at[c, side, pl.ds(yh * 4, 4)]
        return band_ref.at[c, (l + side) % 2, pl.ds(yh * 4, 4)]

    for k, (kind, dy, side) in enumerate(batches):
        for dx in range(4):
            slot = dy * 4 + dx
            if kind == "edge":
                pltpu.make_async_remote_copy(
                    final_edge.at[0], edge_ref.at[core, side, slot], edge_send.at[0, 0], edge_recv.at[side, slot],
                    device_id=sibling, device_id_type=MESH).wait_recv()
            elif (dy, dx, side) != (0, 0, 0):
                band_copy(dy, dx, side).wait_recv()
            else:
                own_band.wait()
        ref = row_of(kind, dy, side, core)
        passes.append(pltpu.make_async_remote_copy(
            ref, ref, pass_send.at[3 + k], pass_recv.at[3 + k], device_id=sibling, device_id_type=MESH))
        passes[-1].start()
    for copy in trace_copies + part_copies + gram_copies + state_copies + edge_copies + band_copies:
        copy.wait_send()
    own_movie.wait()
    for copy in movie_copies:
        copy.wait()
    for k, (kind, dy, side) in enumerate(batches):
        ref = row_of(kind, dy, side, 1 - core)
        pltpu.make_async_remote_copy(
            ref, ref, pass_send.at[3 + k], pass_recv.at[3 + k], device_id=sibling, device_id_type=MESH).wait_recv()
    for copy in passes:
        copy.wait_send()


def product_kernel(planes, movie_ref, band_ref, edge_ref, traces_ref, products_ref, gram_ref):
    z, l, quad, core = position()
    outside = jnp.logical_or(jnp.logical_and(l == 0, z == 0), jnp.logical_and(l == 1, z == planes - 1))
    frames = movie_ref.shape[0] * movie_ref.shape[1] * movie_ref.shape[2] * movie_ref.shape[3]
    movie = movie_ref[...].reshape(frames, movie_ref.shape[4])
    plane = band_ref[...].reshape(frames, 256)
    edge = jnp.where(outside, jnp.zeros((), BF16), edge_ref[...].reshape(frames, 128))
    whole = jnp.concatenate([plane, edge], axis=1)
    plane_at = pl.multiple_of((1 - l) * 128, 128)
    edge_at = pl.multiple_of(l * 256, 128)

    def over_frames(left):
        return lax.dot_general(left, whole, (((0,), (0,)), ((), ())), preferred_element_type=F32)

    products = over_frames(movie)
    products_ref[:, pl.ds(plane_at, 256)] = products[:, :256]
    products_ref[:, pl.ds(edge_at, 128)] = products[:, 256:]
    gram = over_frames(whole)
    gram_ref[pl.ds(plane_at, 256), pl.ds(plane_at, 256)] = gram[:256, :256]
    gram_ref[pl.ds(plane_at, 256), pl.ds(edge_at, 128)] = gram[:256, 256:]
    gram_ref[pl.ds(edge_at, 128), pl.ds(plane_at, 256)] = gram[256:, :256]
    gram_ref[pl.ds(edge_at, 128), pl.ds(edge_at, 128)] = gram[256:, 256:]
    for half in range(2):
        traces_ref[half * 64:half * 64 + 64, :] = band_ref[core, half, quad, :, pl.ds(pl.multiple_of(l * 128, 128), 128)]


def body(planes, frames_data, footprints, traces, counts):
    rows, voxels = frames_data.shape
    share = voxels // 16
    half = rows // 2
    hbm = pl.BlockSpec(memory_space=pl.ANY)
    dma = pltpu.SemaphoreType.DMA
    chunks = voxels // CHUNK
    movie, band, edge = pl.pallas_call(
        functools.partial(exchange_kernel, planes),
        name="exchange",
        out_shape=[
            jax.ShapeDtypeStruct((2, 2, 8, half, share), BF16),
            jax.ShapeDtypeStruct((2, 2, 8, half, 256), BF16),
            jax.ShapeDtypeStruct((2, 2, 8, half, 128), BF16),
        ],
        in_specs=[hbm, hbm, hbm, hbm],
        out_specs=[hbm, hbm, hbm],
        scratch_shapes=[
            pltpu.SMEM((counts.shape[0],), jnp.int32),
            pltpu.VMEM((voxels, 384), BF16), pltpu.VMEM((2, half, voxels), BF16), pltpu.VMEM((6, rows, 128), BF16),
            pltpu.VMEM((384, 384), F32), pltpu.VMEM((rows + 16, 384), F32),
            pltpu.VMEM((2, half + 8, 256), F32), pltpu.VMEM((2, half + 8, 128), F32),
            pltpu.VMEM((half + 8, 256), F32), pltpu.VMEM((2, half + 8, 128), F32),
            pltpu.VMEM((2, 384, 256), BF16), pltpu.VMEM((384, 128), BF16), pltpu.VMEM((2, 384, 128), BF16),
            pltpu.VMEM((768, 256), BF16),
            pltpu.VMEM((ITERS, 3, half, 256), BF16), pltpu.VMEM((half, 256), BF16), pltpu.VMEM((2, half, 128), BF16),
            dma((chunks, 3)), dma((16,)), dma((16,)), dma((5,)), dma((6,)), dma((3,)), dma((3,)),
            dma((3,)), dma((3,)), dma((ITERS, 2)), dma((ITERS, 2)), dma((16,)), dma((16,)),
            dma((2, 8)), dma((2, 8)), dma((11,)), dma((11,)), dma((4,)), pltpu.SemaphoreType.REGULAR,
        ],
        compiler_params=pltpu.CompilerParams(collective_id=0, has_side_effects=True, vmem_limit_bytes=32 << 20),
    )(*[pltpu.with_memory_space_constraint(v, pltpu.HBM) for v in (counts, frames_data.reshape(2, half, voxels), footprints, traces)])
    vmem = pl.BlockSpec(memory_space=pltpu.VMEM)
    return pl.pallas_call(
        functools.partial(product_kernel, planes),
        name="products",
        out_shape=[
            jax.ShapeDtypeStruct((rows, 128), BF16),
            jax.ShapeDtypeStruct((share, 384), F32),
            jax.ShapeDtypeStruct((384, 384), F32),
        ],
        in_specs=[vmem, vmem, vmem],
        out_specs=[vmem, vmem, vmem],
        compiler_params=pltpu.CompilerParams(vmem_limit_bytes=32 << 20),
    )(movie, band, edge)


def solution(mesh):
    return jax.shard_map(
        functools.partial(body, mesh.shape["vox"] // 2),
        mesh=mesh,
        in_specs=(P("tm", "vox"), P("vox", None), P("tm", "vox"), P()),
        out_specs=(P("tm", "vox"), P(("vox", "tm"), None), P("vox", None)),
        check_vma=False,
    )
```

```python
import functools

import jax
import jax.numpy as jnp
from jax import lax
from jax.experimental import pallas as pl
from jax.experimental.pallas import tpu as pltpu
from jax.sharding import PartitionSpec as P

ITERS = 4
CHUNK = 1024
MESH = pl.DeviceIdType.MESH
F32 = jnp.float32
BF16 = jnp.bfloat16


def position():
    vox, tm = lax.axis_index("vox"), lax.axis_index("tm")
    return vox // 2, vox % 2, tm // 2, tm % 2


def turned(quad, dy, dx):
    return ((quad // 4 + dy) % 2) * 4 + (quad % 4 + dx) % 4


def exchange_kernel(
    planes,
    counts_hbm, frames_ref, prints_ref, traces_ref,
    movie_ref, band_ref, edge_ref, products_ref, gram_ref,
    counts_ref, prints, frames, tracebuf, gacc, facc,
    part_plane, part_edge, got_plane, got_edge,
    gram_plane, gram_edge, got_gram, mixing,
    state, final, final_edge,
    load_sem, movie_send, movie_recv, trace_send, trace_recv, part_send, part_recv,
    gram_send, gram_recv, state_send, state_recv, band_send, band_recv,
    edge_send, edge_recv, pass_send, pass_recv, own_sem, met,
):
    z, l, quad, core = position()
    other = 1 - l
    up, down = (z + 1) % planes, (z + planes - 1) % planes
    outward = (z + planes - 1 + 2 * l) % planes
    below, above = z > 0, z < planes - 1
    beside = jnp.where(l == 0, z, planes - 1 - z) > 0
    always = None

    def given(condition, act):
        if condition is None:
            act()
        else:
            pl.when(condition)(act)

    def device(plane, side, q, c):
        return (plane * 2 + side, q * 2 + c)

    me = device(z, l, quad, core)
    across = turned(quad, 1, 0)
    offsets = [(dy, dx) for dy in range(2) for dx in range(4)]
    ring = [(dx, dc) for dx in (1, 3, 2, 0) for dc in range(2) if (dx, dc) != (0, 0)]
    barrier = pltpu.get_barrier_semaphore()
    near = [device(z, l, turned(quad, 0, dx), (core + dc) % 2) for dx, dc in ring]
    near += [device(z, other, quad, core), device(z, l, across, core)]
    near = [(always, target) for target in near]
    near += [(there, device(plane, side, quad, core)) for there, plane in ((above, up), (below, down)) for side in range(2)]

    rows = prints_ref.shape[0]
    chunks = rows // CHUNK
    plane_at = pl.multiple_of((1 - l) * 128, 128)
    edge_at = pl.multiple_of(l * 256, 128)

    def loads(k):
        at = pl.multiple_of(k * CHUNK, CHUNK)
        return (
            pltpu.make_async_copy(prints_ref.at[pl.ds(at, CHUNK), pl.ds(plane_at, 256)], prints.at[pl.ds(at, CHUNK), pl.ds(0, 256)], load_sem.at[k, 0]),
            pltpu.make_async_copy(prints_ref.at[pl.ds(at, CHUNK), pl.ds(edge_at, 128)], prints.at[pl.ds(at, CHUNK), pl.ds(256, 128)], load_sem.at[k, 1]),
            pltpu.make_async_copy(frames_ref.at[:, :, pl.ds(at, CHUNK)], frames.at[:, :, pl.ds(at, CHUNK)], load_sem.at[k, 2]),
        )

    own_counts = pltpu.make_async_copy(counts_hbm, counts_ref, own_sem.at[3])
    own_counts.start()
    for k in range(chunks):
        for copy in loads(k):
            copy.start()
    own_trace = pltpu.make_async_copy(traces_ref, tracebuf.at[2 + l], own_sem.at[0])
    own_trace.start()
    share = movie_ref.shape[4]
    own_movie = pltpu.make_async_copy(
        frames_ref.at[:, :, pl.ds(pl.multiple_of((quad * 2 + core) * share, share), share)],
        movie_ref.at[core, :, quad], own_sem.at[1])
    own_movie.start()
    for there, target in near:
        given(there, functools.partial(pl.semaphore_signal, barrier, inc=1, device_id=target, device_id_type=MESH))

    @pl.when(jnp.logical_not(below))
    def _():
        tracebuf[0:2] = jnp.zeros((2,) + tracebuf.shape[1:], BF16)

    @pl.when(jnp.logical_not(above))
    def _():
        tracebuf[4:6] = jnp.zeros((2,) + tracebuf.shape[1:], BF16)

    gacc[...] = jnp.zeros_like(gacc)
    facc[...] = jnp.zeros_like(facc)
    own_counts.wait()

    def number(tile):
        inside = jnp.logical_and(tile >= 0, tile < 2 * planes)
        return jnp.where(inside, counts_ref[jnp.clip(tile, 0, 2 * planes - 1)], 0)

    numbers = [number(2 * z - 2 + s) for s in range(6)]
    edge_number = jnp.where(l == 0, numbers[1], numbers[4])
    lane = lax.broadcasted_iota(jnp.int32, (1, 128), 1)
    row = lax.broadcasted_iota(jnp.int32, (128, 1), 0)
    live_rows = jnp.concatenate(
        [(row < n).astype(F32) for n in (numbers[2], numbers[3], edge_number)], axis=0)
    live_lanes = [(lane < n).astype(F32) for n in numbers]
    own_live = jnp.concatenate([live_lanes[2], live_lanes[3]], axis=1)

    def chunk_step(k, carry):
        for copy in loads(k):
            copy.wait()
        at = pl.multiple_of(k * CHUNK, CHUNK)
        block = prints[pl.ds(at, CHUNK), :]
        flipped = block.T
        support = jnp.sum(flipped.astype(F32) * live_rows, axis=0, keepdims=True).astype(BF16)
        left = jnp.concatenate(
            [flipped[256:384], frames[0, :, pl.ds(at, CHUNK)], frames[1, :, pl.ds(at, CHUNK)],
             jnp.broadcast_to(support, (16, CHUNK))], axis=0)
        edge = jnp.dot(left, block[:, 256:384], preferred_element_type=F32)
        gacc[256:384, 256:384] += edge[0:128]
        facc[:, 256:384] += edge[128:272]
        left = jnp.concatenate([left, flipped[0:256]], axis=0)
        plane = jnp.dot(left, block[:, 0:256], preferred_element_type=F32)
        gacc[256:384, 0:256] += plane[0:128]
        facc[:, 0:256] += plane[128:272]
        gacc[0:256, 0:256] += plane[272:528]
        return carry

    chunk_step(0, 0)
    pl.semaphore_wait(barrier, len(near) - 4 + 2 * below.astype(jnp.int32) + 2 * above.astype(jnp.int32))
    pl.semaphore_signal(met, inc=1, device_id=device(z, l, across, core), device_id_type=MESH)

    def to(src, dst, send, recv, plane, side, q=None):
        return pltpu.make_async_remote_copy(
            src, dst, send, recv, device_id=device(plane, side, quad if q is None else q, core), device_id_type=MESH)

    sent = []

    def send(there, copy):
        given(there, copy.start)
        sent.append((there, copy))

    for k, (there, plane, side, slot) in enumerate(
            [(always, z, other, 2 + l), (above, up, 0, l), (above, up, 1, l), (below, down, 0, 4 + l), (below, down, 1, 4 + l)]):
        send(there, to(traces_ref, tracebuf.at[slot], trace_send.at[k], trace_recv.at[slot], plane, side))

    def movie_copy(dy, dx, dc):
        q, c = turned(quad, dy, dx), (core + dc) % 2
        slot = (dy * 4 + dx) * 2 + dc
        return pltpu.make_async_remote_copy(
            frames_ref.at[:, :, pl.ds(pl.multiple_of((q * 2 + c) * share, share), share)],
            movie_ref.at[core, :, quad], movie_send.at[slot], movie_recv.at[slot],
            device_id=device(z, l, q, c), device_id_type=MESH)

    lax.fori_loop(1, chunks, chunk_step, 0)

    gacc[0:256, 256:384] = gacc[256:384, 0:256].T
    gram = gacc[...]
    high = gram.astype(BF16)
    low = (gram - high.astype(F32)).astype(BF16)
    gram_plane[l] = high[:, :256]
    gram_edge[...] = high[:, 256:]

    own_trace.wait()
    for there, slot in ((below, 0), (below, 1), (above, 4), (above, 5), (always, 2 + other)):
        given(there, to(traces_ref, tracebuf.at[slot], trace_send.at[0], trace_recv.at[slot], z, other).wait_recv)

    def trace(slot, live):
        return (tracebuf[slot].astype(F32) * live).astype(BF16)

    edge_live = jnp.where(l == 0, live_lanes[1], live_lanes[4])
    band = jnp.concatenate(
        [trace(2, live_lanes[2]), trace(3, live_lanes[3]), trace(1 + 3 * l, edge_live)], axis=1)
    reach = facc[128:136, :]
    parts = facc[0:128, :] - jnp.dot(band, high, preferred_element_type=F32) - jnp.dot(band, low, preferred_element_type=F32)
    for half in range(2):
        piece = jnp.concatenate([parts[half * 64:half * 64 + 64], reach], axis=0)
        part_plane[half] = piece[:, :256]
        part_edge[half] = piece[:, 256:]
    pl.semaphore_wait(met, 1)

    send(always, to(part_plane.at[other], got_plane, part_send.at[0], part_recv.at[2], z, other))
    send(beside, to(part_edge.at[other], got_edge.at[other], part_send.at[2], part_recv.at[other], outward, other))
    send(beside, to(part_edge.at[l], got_edge.at[other], part_send.at[1], part_recv.at[other], outward, l))
    own_rows = pl.ds(pl.multiple_of(core * 192, 64), 192)
    send(always, to(gram_plane.at[l, own_rows], gram_plane.at[l, own_rows], gram_send.at[0], gram_recv.at[2], z, other, across))
    send(beside, to(gram_edge.at[own_rows], got_gram.at[other, own_rows], gram_send.at[2], gram_recv.at[other], outward, other, across))
    send(beside, to(gram_edge.at[own_rows], got_gram.at[other, own_rows], gram_send.at[1], gram_recv.at[other], outward, l))
    movie_copies = [movie_copy(0, dx, dc) for dx, dc in ring]
    for copy in movie_copies:
        copy.start()

    mine = pl.ds(pl.multiple_of(l * 64, 64), 64)
    for s in range(6):
        value = (tracebuf[s, mine, :].astype(F32) * live_lanes[s]).astype(BF16)
        state[0, s // 2, :, (s % 2) * 128:(s % 2) * 128 + 128] = value

    to(part_plane.at[0], got_plane, part_send.at[0], part_recv.at[2], z, other).wait_recv()
    for there, slot in ((below, 0), (above, 1)):
        given(there, to(part_edge.at[0], got_edge.at[slot], part_send.at[0], part_recv.at[slot], z, other).wait_recv)
    total = part_plane[l] + got_plane[...] + jnp.concatenate(
        [jnp.where(below, got_edge[0], 0.0), jnp.where(above, got_edge[1], 0.0)], axis=1)
    slope = total[0:64]
    majorant = jnp.maximum(total[64:65], 1.0)

    def updated(current, slope):
        value = jnp.maximum(current.astype(F32) + slope / majorant, 0.0)
        return (value * own_live).astype(BF16)

    def send_state(step):
        send(above, to(state.at[step, 1], state.at[step, 0], state_send.at[step, 0], state_recv.at[step, 0], up, l))
        send(below, to(state.at[step, 1], state.at[step, 2], state_send.at[step, 1], state_recv.at[step, 1], down, l))

    state[1, 1] = updated(state[0, 1], slope)
    send_state(1)

    late_movie = [movie_copy(1, dx, dc) for dx in (0, 2, 1, 3) for dc in range(2)]
    for copy in late_movie:
        copy.start()
    movie_copies += late_movie

    sibling = (z * 2 + l, quad * 2 + 1 - core)

    def gram_pass(k, refs):
        ref = refs(own_rows)
        return pltpu.make_async_remote_copy(
            ref, ref, pass_send.at[k], pass_recv.at[k], device_id=sibling, device_id_type=MESH)

    gram_parts = [
        (always, 2, lambda part: gram_plane.at[other, part]),
        (below, 0, lambda part: got_gram.at[0, part]),
        (above, 1, lambda part: got_gram.at[1, part]),
    ]
    for there, k, refs in gram_parts:
        given(there, to(refs(own_rows), refs(own_rows), gram_send.at[0], gram_recv.at[k], z, other).wait_recv)
        send(there, gram_pass(k, refs))
    its_rows = pl.ds(pl.multiple_of((1 - core) * 192, 64), 192)
    for there, k, refs in gram_parts:
        given(there, pltpu.make_async_remote_copy(
            refs(its_rows), refs(its_rows), pass_send.at[k], pass_recv.at[k], device_id=sibling, device_id_type=MESH).wait_recv)
    ga, gb = gram_plane[0].astype(F32), gram_plane[1].astype(F32)
    gc = jnp.where(below, got_gram[0].astype(F32), 0.0)
    gd = jnp.where(above, got_gram[1].astype(F32), 0.0)
    mixing[0:128, 0:128] = gc[0:128].astype(BF16)
    mixing[0:128, 128:256] = jnp.zeros((128, 128), BF16)
    mixing[128:256, 0:128] = (gc[128:256] + ga[256:384, 0:128]).astype(BF16)
    mixing[128:256, 128:256] = ga[256:384, 128:256].astype(BF16)
    mixing[256:384, 0:128] = (gc[256:384] + ga[0:128, 0:128] + gb[0:128, 0:128]).astype(BF16)
    mixing[256:384, 128:256] = (ga[0:128, 128:256] + gb[0:128, 128:256]).astype(BF16)
    mixing[384:512, 0:128] = (ga[128:256, 0:128] + gb[128:256, 0:128]).astype(BF16)
    mixing[384:512, 128:256] = (ga[128:256, 128:256] + gb[128:256, 128:256] + gd[256:384]).astype(BF16)
    mixing[512:640, 0:128] = gb[256:384, 0:128].astype(BF16)
    mixing[512:640, 128:256] = (gb[256:384, 128:256] + gd[0:128]).astype(BF16)
    mixing[640:768, 0:128] = jnp.zeros((128, 128), BF16)
    mixing[640:768, 128:256] = gd[128:256].astype(BF16)

    def mixed_own(step):
        return jnp.dot(state[step, 1], mixing[256:512], preferred_element_type=F32)

    def mixed_next(step):
        left = jnp.where(below, state[step, 0], jnp.zeros((), BF16))
        right = jnp.where(above, state[step, 2], jnp.zeros((), BF16))
        return (jnp.dot(left, mixing[0:256], preferred_element_type=F32)
                + jnp.dot(right, mixing[512:768], preferred_element_type=F32))

    base = slope + mixed_own(0) + mixed_next(0)
    for step in range(1, ITERS):
        partial = base - mixed_own(step)
        for there, side, slot in ((below, 0, 0), (above, 1, 2)):
            given(there, to(state.at[step, 1], state.at[step, slot], state_send.at[step, side], state_recv.at[step, side], z, other).wait_recv)
        value = updated(state[step, 1], partial - mixed_next(step))
        if step < ITERS - 1:
            state[step + 1, 1] = value
            send_state(step + 1)
        else:
            final[...] = value
            final_edge[0] = value[:, :128]
            final_edge[1] = value[:, 128:]

    def band_copy(dy, dx, dl):
        slot = (dy * 4 + dx) * 2 + dl
        return pltpu.make_async_remote_copy(
            final, band_ref.at[core, l, quad], band_send.at[slot], band_recv.at[slot],
            device_id=device(z, (l + dl) % 2, turned(quad, dy, dx), core), device_id_type=MESH)

    def edge_copy(dy, dx, side):
        slot = dy * 4 + dx
        return pltpu.make_async_remote_copy(
            final_edge.at[1 - side], edge_ref.at[core, l, quad], edge_send.at[side, slot], edge_recv.at[l, slot],
            device_id=device(up if side == 0 else down, side, turned(quad, dy, dx), core), device_id_type=MESH)

    own_band = pltpu.make_async_copy(final, band_ref.at[core, l, quad], own_sem.at[2])
    own_band.start()
    batches = [("edge", 1, 0), ("band", 1, 0), ("edge", 1, 1), ("band", 0, 1), ("edge", 0, 0), ("band", 1, 1), ("edge", 0, 1), ("band", 0, 0)]
    for kind, dy, side in batches:
        for dx in (2, 1, 3, 0):
            if kind == "edge":
                send(above if side == 0 else below, edge_copy(dy, dx, side))
            elif (dy, dx, side) != (0, 0, 0):
                send(always, band_copy(dy, dx, side))

    def row_of(kind, dy, side, c):
        yh = (quad // 4 + dy) % 2
        if kind == "edge":
            return edge_ref.at[c, side, pl.ds(yh * 4, 4)]
        return band_ref.at[c, (l + side) % 2, pl.ds(yh * 4, 4)]

    own_movie.wait()
    for copy in movie_copies:
        copy.wait_recv()
    for k, (kind, dy, side) in enumerate(batches):
        there = beside if kind == "edge" else always
        for dx in range(4):
            slot = dy * 4 + dx
            if kind == "edge":
                given(there, pltpu.make_async_remote_copy(
                    final_edge.at[0], edge_ref.at[core, side, slot], edge_send.at[0, 0], edge_recv.at[side, slot],
                    device_id=sibling, device_id_type=MESH).wait_recv)
            elif (dy, dx, side) != (0, 0, 0):
                band_copy(dy, dx, side).wait_recv()
            else:
                own_band.wait()
        ref = row_of(kind, dy, side, core)
        send(there, pltpu.make_async_remote_copy(
            ref, ref, pass_send.at[3 + k], pass_recv.at[3 + k], device_id=sibling, device_id_type=MESH))

    partial_products(beside, movie_ref.at[core], band_ref.at[core], edge_ref.at[core], products_ref, gram_ref)

    for there, copy in sent:
        given(there, copy.wait_send)
    for copy in movie_copies:
        copy.wait_send()
    for k, (kind, dy, side) in enumerate(batches):
        ref = row_of(kind, dy, side, 1 - core)
        given(beside if kind == "edge" else always, pltpu.make_async_remote_copy(
            ref, ref, pass_send.at[3 + k], pass_recv.at[3 + k], device_id=sibling, device_id_type=MESH).wait_recv)


def partial_products(beside, movie_ref, band_ref, edge_ref, products_ref, gram_ref):
    frames = movie_ref.shape[0] * movie_ref.shape[1] * movie_ref.shape[2]
    movie = movie_ref[...].reshape(frames, movie_ref.shape[3])
    plane = band_ref[...].reshape(frames, 256)
    edge = jnp.where(beside, edge_ref[...].reshape(frames, 128), jnp.zeros((), BF16))
    whole = jnp.concatenate([plane, edge], axis=1)

    def over_frames(left):
        return lax.dot_general(left, whole, (((0,), (0,)), ((), ())), preferred_element_type=F32)

    products_ref[...] = over_frames(movie)
    gram_ref[...] = over_frames(whole)


def product_kernel(planes, movie_ref, band_ref, edge_ref, products_in, gram_in, traces_ref, products_ref, gram_ref, products, gram):
    z, l, quad, core = position()
    beside = jnp.where(l == 0, z, planes - 1 - z) > 0
    its = 1 - core
    partial_products(beside, movie_ref.at[its], band_ref.at[its], edge_ref.at[its], products, gram)
    plane_at = pl.multiple_of((1 - l) * 128, 128)
    edge_at = pl.multiple_of(l * 256, 128)
    products_ref[:, pl.ds(plane_at, 256)] = products[:, :256] + products_in[:, :256]
    products_ref[:, pl.ds(edge_at, 128)] = products[:, 256:] + products_in[:, 256:]
    for at, rows in ((plane_at, slice(0, 256)), (edge_at, slice(256, 384))):
        gram_ref[pl.ds(at, rows.stop - rows.start), pl.ds(plane_at, 256)] = gram[rows, :256] + gram_in[rows, :256]
        gram_ref[pl.ds(at, rows.stop - rows.start), pl.ds(edge_at, 128)] = gram[rows, 256:] + gram_in[rows, 256:]
    for half in range(2):
        traces_ref[half * 64:half * 64 + 64, :] = band_ref[core, half, quad, :, pl.ds(pl.multiple_of(l * 128, 128), 128)]


def body(planes, frames_data, footprints, traces, counts):
    rows, voxels = frames_data.shape
    share = voxels // 16
    half = rows // 2
    hbm = pl.BlockSpec(memory_space=pl.ANY)
    dma = pltpu.SemaphoreType.DMA
    chunks = voxels // CHUNK
    gathered = pl.pallas_call(
        functools.partial(exchange_kernel, planes),
        name="exchange",
        out_shape=[
            jax.ShapeDtypeStruct((2, 2, 8, half, share), BF16),
            jax.ShapeDtypeStruct((2, 2, 8, half, 256), BF16),
            jax.ShapeDtypeStruct((2, 2, 8, half, 128), BF16),
            jax.ShapeDtypeStruct((share, 384), F32),
            jax.ShapeDtypeStruct((384, 384), F32),
        ],
        in_specs=[hbm, hbm, hbm, hbm],
        out_specs=[pl.BlockSpec(memory_space=pltpu.VMEM)] * 5,
        scratch_shapes=[
            pltpu.SMEM((counts.shape[0],), jnp.int32),
            pltpu.VMEM((voxels, 384), BF16), pltpu.VMEM((2, half, voxels), BF16), pltpu.VMEM((6, rows, 128), BF16),
            pltpu.VMEM((384, 384), F32), pltpu.VMEM((rows + 16, 384), F32),
            pltpu.VMEM((2, half + 8, 256), F32), pltpu.VMEM((2, half + 8, 128), F32),
            pltpu.VMEM((half + 8, 256), F32), pltpu.VMEM((2, half + 8, 128), F32),
            pltpu.VMEM((2, 384, 256), BF16), pltpu.VMEM((384, 128), BF16), pltpu.VMEM((2, 384, 128), BF16),
            pltpu.VMEM((768, 256), BF16),
            pltpu.VMEM((ITERS, 3, half, 256), BF16), pltpu.VMEM((half, 256), BF16), pltpu.VMEM((2, half, 128), BF16),
            dma((chunks, 3)), dma((16,)), dma((16,)), dma((5,)), dma((6,)), dma((3,)), dma((3,)),
            dma((3,)), dma((3,)), dma((ITERS, 2)), dma((ITERS, 2)), dma((16,)), dma((16,)),
            dma((2, 8)), dma((2, 8)), dma((11,)), dma((11,)), dma((4,)), pltpu.SemaphoreType.REGULAR,
        ],
        compiler_params=pltpu.CompilerParams(collective_id=0, has_side_effects=True, vmem_limit_bytes=32 << 20),
    )(*[pltpu.with_memory_space_constraint(v, pltpu.HBM) for v in (counts, frames_data.reshape(2, half, voxels), footprints, traces)])
    vmem = pl.BlockSpec(memory_space=pltpu.VMEM)
    return pl.pallas_call(
        functools.partial(product_kernel, planes),
        name="products",
        out_shape=[
            jax.ShapeDtypeStruct((rows, 128), BF16),
            jax.ShapeDtypeStruct((share, 384), F32),
            jax.ShapeDtypeStruct((384, 384), F32),
        ],
        in_specs=[vmem] * 5,
        out_specs=[vmem] * 3,
        scratch_shapes=[pltpu.VMEM((share, 384), F32), pltpu.VMEM((384, 384), F32)],
        compiler_params=pltpu.CompilerParams(vmem_limit_bytes=32 << 20),
    )(*gathered)


def solution(mesh):
    return jax.shard_map(
        functools.partial(body, mesh.shape["vox"] // 2),
        mesh=mesh,
        in_specs=(P("tm", "vox"), P("vox", None), P("tm", "vox"), P()),
        out_specs=(P("tm", "vox"), P(("vox", "tm"), None), P("vox", None)),
        check_vma=False,
    )
```

```python
import functools

import jax
import jax.numpy as jnp
from jax import lax
from jax.experimental import pallas as pl
from jax.experimental.pallas import tpu as pltpu
from jax.sharding import PartitionSpec as P

ITERS = 4
CHUNK = 1024
MESH = pl.DeviceIdType.MESH
F32 = jnp.float32
BF16 = jnp.bfloat16


def position():
    vox, tm = lax.axis_index("vox"), lax.axis_index("tm")
    return vox // 2, vox % 2, tm // 2, tm % 2


def turned(quad, dy, dx):
    return ((quad // 4 + dy) % 2) * 4 + (quad % 4 + dx) % 4


def exchange_kernel(
    planes,
    counts_hbm, frames_ref, prints_ref, traces_ref,
    movie_ref, band_ref, edge_ref, products_ref, gram_ref,
    counts_ref, prints, lefts, tracebuf, sums,
    part_plane, part_edge, got_plane, got_edge,
    gram_plane, gram_edge, got_gram, mixing,
    state, final, final_edge,
    load_sem, movie_send, movie_recv, trace_send, trace_recv, part_send, part_recv,
    gram_send, gram_recv, state_send, state_recv, band_send, band_recv,
    edge_send, edge_recv, pass_send, pass_recv, own_sem, met,
):
    z, l, quad, core = position()
    other = 1 - l
    up, down = (z + 1) % planes, (z + planes - 1) % planes
    outward = (z + planes - 1 + 2 * l) % planes
    below, above = z > 0, z < planes - 1
    beside = jnp.where(l == 0, z, planes - 1 - z) > 0
    always = None

    def given(condition, act):
        if condition is None:
            act()
        else:
            pl.when(condition)(act)

    def device(plane, side, q, c):
        return (plane * 2 + side, q * 2 + c)

    me = device(z, l, quad, core)
    across = turned(quad, 1, 0)
    offsets = [(dy, dx) for dy in range(2) for dx in range(4)]
    ring = [(dx, dc) for dx in (1, 3, 2, 0) for dc in range(2) if (dx, dc) != (0, 0)]
    barrier = pltpu.get_barrier_semaphore()
    near = [(always, device(z, other, quad, core))]
    near += [(there, device(plane, side, quad, core)) for there, plane in ((above, up), (below, down)) for side in range(2)]
    near += [(always, device(z, l, across, core))]
    near += [(always, device(z, l, turned(quad, 0, dx), (core + dc) % 2)) for dx, dc in ring]

    rows = prints_ref.shape[0]
    chunks = rows // CHUNK
    plane_at = pl.multiple_of((1 - l) * 128, 128)
    edge_at = pl.multiple_of(l * 256, 128)

    def loads(k):
        at = pl.multiple_of(k * CHUNK, CHUNK)
        return (
            pltpu.make_async_copy(prints_ref.at[pl.ds(at, CHUNK), pl.ds(plane_at, 256)], prints.at[pl.ds(at, CHUNK), pl.ds(0, 256)], load_sem.at[k, 0]),
            pltpu.make_async_copy(prints_ref.at[pl.ds(at, CHUNK), pl.ds(edge_at, 128)], prints.at[pl.ds(at, CHUNK), pl.ds(256, 128)], load_sem.at[k, 1]),
            pltpu.make_async_copy(frames_ref.at[0, :, pl.ds(at, CHUNK)], lefts.at[128:192, pl.ds(at, CHUNK)], load_sem.at[k, 2]),
            pltpu.make_async_copy(frames_ref.at[1, :, pl.ds(at, CHUNK)], lefts.at[192:256, pl.ds(at, CHUNK)], load_sem.at[k, 3]),
        )

    own_counts = pltpu.make_async_copy(counts_hbm, counts_ref, own_sem.at[3])
    own_counts.start()
    for k in range(chunks):
        for copy in loads(k):
            copy.start()
    own_trace = pltpu.make_async_copy(traces_ref, tracebuf.at[2 + l], own_sem.at[0])
    own_trace.start()
    share = movie_ref.shape[4]
    own_movie = pltpu.make_async_copy(
        frames_ref.at[:, :, pl.ds(pl.multiple_of((quad * 2 + core) * share, share), share)],
        movie_ref.at[core, :, quad], own_sem.at[1])
    own_movie.start()
    for there, target in near:
        given(there, functools.partial(pl.semaphore_signal, barrier, inc=1, device_id=target, device_id_type=MESH))

    @pl.when(jnp.logical_not(below))
    def _():
        tracebuf[0:2] = jnp.zeros((2,) + tracebuf.shape[1:], BF16)
        for step in range(1, ITERS):
            state[step, 0] = jnp.zeros(state.shape[2:], BF16)

    @pl.when(jnp.logical_not(above))
    def _():
        tracebuf[4:6] = jnp.zeros((2,) + tracebuf.shape[1:], BF16)
        for step in range(1, ITERS):
            state[step, 2] = jnp.zeros(state.shape[2:], BF16)

    @pl.when(jnp.logical_not(beside))
    def _():
        edge_ref[...] = jnp.zeros_like(edge_ref)

    own_counts.wait()

    def number(tile):
        inside = jnp.logical_and(tile >= 0, tile < 2 * planes)
        return jnp.where(inside, counts_ref[jnp.clip(tile, 0, 2 * planes - 1)], 0)

    numbers = [number(2 * z - 2 + s) for s in range(6)]
    edge_number = jnp.where(l == 0, numbers[1], numbers[4])
    lane = lax.broadcasted_iota(jnp.int32, (1, 128), 1)
    row = lax.broadcasted_iota(jnp.int32, (128, 1), 0)
    live_rows = jnp.concatenate(
        [(row < n).astype(F32) for n in (numbers[2], numbers[3], edge_number)], axis=0)
    live_lanes = [(lane < n).astype(F32) for n in numbers]
    own_live = jnp.concatenate([live_lanes[2], live_lanes[3]], axis=1)

    def turn(k):
        for copy in loads(k):
            copy.wait()
        at = pl.multiple_of(k * CHUNK, CHUNK)
        flipped = prints[pl.ds(at, CHUNK), :].T
        support = jnp.sum(flipped.astype(F32) * live_rows, axis=0, keepdims=True).astype(BF16)
        lefts[0:128, pl.ds(at, CHUNK)] = flipped[256:384]
        lefts[256:272, pl.ds(at, CHUNK)] = jnp.broadcast_to(support, (16, CHUNK))
        lefts[272:528, pl.ds(at, CHUNK)] = flipped[0:256]

    turn(0)
    pl.semaphore_wait(barrier, len(near) - 4 + 2 * below.astype(jnp.int32) + 2 * above.astype(jnp.int32))
    pl.semaphore_signal(met, inc=1, device_id=device(z, l, across, core), device_id_type=MESH)

    def to(src, dst, send, recv, plane, side, q=None):
        return pltpu.make_async_remote_copy(
            src, dst, send, recv, device_id=device(plane, side, quad if q is None else q, core), device_id_type=MESH)

    sent = []

    def send(there, copy):
        given(there, copy.start)
        sent.append((there, copy))

    send(always, to(traces_ref, tracebuf.at[2 + l], trace_send.at[0], trace_recv.at[2 + l], z, other))
    send(beside, to(traces_ref, tracebuf.at[4 - 3 * l], trace_send.at[1], trace_recv.at[4 - 3 * l], outward, other))

    inward = (z + planes + 1 - 2 * l) % planes
    half_rows = [pl.ds(pl.multiple_of(side * 64, 64), 64) for side in (l, other)]

    def trace_rows(k, plane, side, slot, part):
        return to(
            traces_ref.at[part], tracebuf.at[slot, part], trace_send.at[k], trace_recv.at[slot], plane, side)

    def movie_copy(dy, dx, dc):
        q, c = turned(quad, dy, dx), (core + dc) % 2
        slot = (dy * 4 + dx) * 2 + dc
        return pltpu.make_async_remote_copy(
            frames_ref.at[:, :, pl.ds(pl.multiple_of((q * 2 + c) * share, share), share)],
            movie_ref.at[core, :, quad], movie_send.at[slot], movie_recv.at[slot],
            device_id=device(z, l, q, c), device_id_type=MESH)

    movie_copies = [movie_copy(0, dx, dc) for dx, dc in ring]
    for copy in movie_copies:
        copy.start()
    for k in range(1, chunks):
        turn(k)
    sums[0:272, 256:384] = jnp.dot(lefts[0:272], prints[:, 256:384], preferred_element_type=F32)
    sums[:, 0:256] = jnp.dot(lefts[...], prints[:, 0:256], preferred_element_type=F32)

    sums[272:528, 256:384] = sums[0:128, 0:256].T
    gram = jnp.concatenate([sums[272:528, :], sums[0:128, :]], axis=0)
    high = gram.astype(BF16)
    low = (gram - high.astype(F32)).astype(BF16)
    gram_plane[l] = high[:, :256]
    gram_edge[...] = high[:, 256:]

    own_trace.wait()
    for there, slot in ((always, 2 + other), (beside, 1 + 3 * l)):
        given(there, to(traces_ref, tracebuf.at[slot], trace_send.at[0], trace_recv.at[slot], z, other).wait_recv)

    def trace(slot, live):
        return (tracebuf[slot].astype(F32) * live).astype(BF16)

    edge_live = jnp.where(l == 0, live_lanes[1], live_lanes[4])
    band = jnp.concatenate(
        [trace(2, live_lanes[2]), trace(3, live_lanes[3]), trace(1 + 3 * l, edge_live)], axis=1)
    reach = sums[256:264, :]
    parts = sums[128:256, :] - jnp.dot(
        jnp.concatenate([band, band], axis=1), jnp.concatenate([high, low], axis=0), preferred_element_type=F32)
    for half in range(2):
        piece = jnp.concatenate([parts[half * 64:half * 64 + 64], reach], axis=0)
        part_plane[half] = piece[:, :256]
        part_edge[half] = piece[:, 256:]
    pl.semaphore_wait(met, 1)

    send(always, to(part_plane.at[other], got_plane, part_send.at[0], part_recv.at[2], z, other))
    send(beside, to(part_edge.at[other], got_edge.at[other], part_send.at[2], part_recv.at[other], outward, other))
    send(beside, to(part_edge.at[l], got_edge.at[other], part_send.at[1], part_recv.at[other], outward, l))
    own_rows = pl.ds(pl.multiple_of(core * 192, 64), 192)
    send(always, to(gram_plane.at[l, own_rows], gram_plane.at[l, own_rows], gram_send.at[0], gram_recv.at[2], z, other, across))
    send(beside, to(gram_edge.at[own_rows], got_gram.at[other, own_rows], gram_send.at[2], gram_recv.at[other], outward, other, across))
    send(beside, to(gram_edge.at[own_rows], got_gram.at[other, own_rows], gram_send.at[1], gram_recv.at[other], outward, l))


    send(above, trace_rows(2, up, l, l, half_rows[0]))
    send(below, trace_rows(3, down, l, 4 + l, half_rows[0]))
    send(jnp.where(l == 0, z < planes - 1, z > 0), trace_rows(4, inward, other, 5 * l, half_rows[1]))
    to(part_plane.at[0], got_plane, part_send.at[0], part_recv.at[2], z, other).wait_recv()
    for there, slot in ((below, 0), (above, 1)):
        given(there, to(part_edge.at[0], got_edge.at[slot], part_send.at[0], part_recv.at[slot], z, other).wait_recv)
    total = part_plane[l] + got_plane[...] + jnp.concatenate(
        [jnp.where(below, got_edge[0], 0.0), jnp.where(above, got_edge[1], 0.0)], axis=1)
    slope = total[0:64]
    majorant = jnp.maximum(total[64:65], 1.0)

    def updated(current, slope):
        value = jnp.maximum(current.astype(F32) + slope / majorant, 0.0)
        return (value * own_live).astype(BF16)

    def send_state(step):
        send(above, to(state.at[step, 1], state.at[step, 0], state_send.at[step, 0], state_recv.at[step, 0], up, l))
        send(below, to(state.at[step, 1], state.at[step, 2], state_send.at[step, 1], state_recv.at[step, 1], down, l))

    mine = half_rows[0]

    def start_state(slots):
        for s in slots:
            value = (tracebuf[s, mine, :].astype(F32) * live_lanes[s]).astype(BF16)
            state[0, s // 2, :, (s % 2) * 128:(s % 2) * 128 + 128] = value

    start_state((2, 3))
    state[1, 1] = updated(state[0, 1], slope)
    send_state(1)

    late_movie = [movie_copy(1, dx, dc) for dc in range(2) for dx in (2, 1, 3, 0)]
    for copy in late_movie:
        copy.start()
    movie_copies += late_movie

    for there, slot in ((below, l), (above, 4 + l), (jnp.where(l == 0, z < planes - 1, z > 0), 5 - 5 * l)):
        given(there, trace_rows(2, z, other, slot, half_rows[0]).wait_recv)
    start_state((0, 1, 4, 5))

    sibling = (z * 2 + l, quad * 2 + 1 - core)

    def gram_pass(k, refs):
        ref = refs(own_rows)
        return pltpu.make_async_remote_copy(
            ref, ref, pass_send.at[k], pass_recv.at[k], device_id=sibling, device_id_type=MESH)

    gram_parts = [
        (always, 2, lambda part: gram_plane.at[other, part]),
        (below, 0, lambda part: got_gram.at[0, part]),
        (above, 1, lambda part: got_gram.at[1, part]),
    ]
    for there, k, refs in gram_parts:
        given(there, to(refs(own_rows), refs(own_rows), gram_send.at[0], gram_recv.at[k], z, other).wait_recv)
        send(there, gram_pass(k, refs))
    its_rows = pl.ds(pl.multiple_of((1 - core) * 192, 64), 192)
    for there, k, refs in gram_parts:
        given(there, pltpu.make_async_remote_copy(
            refs(its_rows), refs(its_rows), pass_send.at[k], pass_recv.at[k], device_id=sibling, device_id_type=MESH).wait_recv)
    ga, gb = gram_plane[0].astype(F32), gram_plane[1].astype(F32)
    gc = jnp.where(below, got_gram[0].astype(F32), 0.0)
    gd = jnp.where(above, got_gram[1].astype(F32), 0.0)
    mixing[0:128, 0:128] = gc[0:128].astype(BF16)
    mixing[0:128, 128:256] = jnp.zeros((128, 128), BF16)
    mixing[128:256, 0:128] = (gc[128:256] + ga[256:384, 0:128]).astype(BF16)
    mixing[128:256, 128:256] = ga[256:384, 128:256].astype(BF16)
    mixing[256:384, 0:128] = (gc[256:384] + ga[0:128, 0:128] + gb[0:128, 0:128]).astype(BF16)
    mixing[256:384, 128:256] = (ga[0:128, 128:256] + gb[0:128, 128:256]).astype(BF16)
    mixing[384:512, 0:128] = (ga[128:256, 0:128] + gb[128:256, 0:128]).astype(BF16)
    mixing[384:512, 128:256] = (ga[128:256, 128:256] + gb[128:256, 128:256] + gd[256:384]).astype(BF16)
    mixing[512:640, 0:128] = gb[256:384, 0:128].astype(BF16)
    mixing[512:640, 128:256] = (gb[256:384, 128:256] + gd[0:128]).astype(BF16)
    mixing[640:768, 0:128] = jnp.zeros((128, 128), BF16)
    mixing[640:768, 128:256] = gd[128:256].astype(BF16)

    def arrived(step):
        for there, side, slot in ((below, 0, 0), (above, 1, 2)):
            given(there, to(state.at[step, 1], state.at[step, slot], state_send.at[step, side], state_recv.at[step, side], z, other).wait_recv)

    base = slope
    for step in range(1, ITERS):
        first = 0 if step == 1 else step
        own = jnp.dot(
            jnp.concatenate([state[k, 1] for k in range(first, step + 1)], axis=0), mixing[256:512], preferred_element_type=F32)
        arrived(step)
        mix = own
        for slot in (0, 2):
            sides = jnp.concatenate([state[k, slot] for k in range(first, step + 1)], axis=0)
            mix = mix + jnp.dot(sides, mixing[slot * 256:slot * 256 + 256], preferred_element_type=F32)
        if step == 1:
            base = base + mix[:64]
            mix = mix[64:]
        value = updated(state[step, 1], base - mix)
        if step < ITERS - 1:
            state[step + 1, 1] = value
            send_state(step + 1)
        else:
            final[...] = value
            final_edge[0] = value[:, :128]
            final_edge[1] = value[:, 128:]

    def band_copy(dy, dx, dl):
        slot = (dy * 4 + dx) * 2 + dl
        return pltpu.make_async_remote_copy(
            final, band_ref.at[core, l, quad], band_send.at[slot], band_recv.at[slot],
            device_id=device(z, (l + dl) % 2, turned(quad, dy, dx), core), device_id_type=MESH)

    def edge_copy(dy, dx, side):
        slot = dy * 4 + dx
        return pltpu.make_async_remote_copy(
            final_edge.at[1 - side], edge_ref.at[core, l, quad], edge_send.at[side, slot], edge_recv.at[l, slot],
            device_id=device(up if side == 0 else down, side, turned(quad, dy, dx), core), device_id_type=MESH)

    own_band = pltpu.make_async_copy(final, band_ref.at[core, l, quad], own_sem.at[2])
    own_band.start()
    batches = [("edge", 1, 0), ("edge", 1, 1), ("band", 1, 0), ("band", 1, 1), ("edge", 0, 0), ("edge", 0, 1), ("band", 0, 1), ("band", 0, 0)]
    for kind, dy, side in batches:
        for dx in (2, 1, 3, 0):
            if kind == "edge":
                send(above if side == 0 else below, edge_copy(dy, dx, side))
            elif (dy, dx, side) != (0, 0, 0):
                send(always, band_copy(dy, dx, side))

    def row_of(kind, dy, side, c):
        yh = (quad // 4 + dy) % 2
        if kind == "edge":
            return edge_ref.at[c, side, pl.ds(yh * 4, 4)]
        return band_ref.at[c, (l + side) % 2, pl.ds(yh * 4, 4)]

    for k, (kind, dy, side) in enumerate(batches):
        there = beside if kind == "edge" else always
        for dx in range(4):
            slot = dy * 4 + dx
            if kind == "edge":
                given(there, pltpu.make_async_remote_copy(
                    final_edge.at[0], edge_ref.at[core, side, slot], edge_send.at[0, 0], edge_recv.at[side, slot],
                    device_id=sibling, device_id_type=MESH).wait_recv)
            elif (dy, dx, side) != (0, 0, 0):
                band_copy(dy, dx, side).wait_recv()
            else:
                own_band.wait()
        ref = row_of(kind, dy, side, core)
        send(there, pltpu.make_async_remote_copy(
            ref, ref, pass_send.at[3 + k], pass_recv.at[3 + k], device_id=sibling, device_id_type=MESH))

    def passed(k):
        kind, dy, side = batches[k]
        ref = row_of(kind, dy, side, 1 - core)
        given(beside if kind == "edge" else always, pltpu.make_async_remote_copy(
            ref, ref, pass_send.at[3 + k], pass_recv.at[3 + k], device_id=sibling, device_id_type=MESH).wait_recv)

    own_movie.wait()
    for copy in movie_copies:
        copy.wait_recv()
    every = slice(None)
    products_ref[...], gram_ref[...] = partial_products(core, every, movie_ref, band_ref, edge_ref)
    for k in range(4):
        passed(k)
    products, gram = partial_products(1 - core, row_slice(across), movie_ref, band_ref, edge_ref)
    products_ref[...] += products
    gram_ref[...] += gram
    for k in range(4, 8):
        passed(k)
    for there, copy in sent:
        given(there, copy.wait_send)
    for copy in movie_copies:
        copy.wait_send()


def row_slice(quad):
    return pl.ds(quad // 4 * 4, 4)


def partial_products(core, row, movie_ref, band_ref, edge_ref):
    def frames_of(ref):
        return ref[core, :, row].reshape(-1, ref.shape[-1])

    whole = jnp.concatenate([frames_of(band_ref), frames_of(edge_ref)], axis=1)

    def over_frames(left):
        return lax.dot_general(left, whole, (((0,), (0,)), ((), ())), preferred_element_type=F32)

    return over_frames(frames_of(movie_ref)), over_frames(whole)


def product_kernel(movie_ref, band_ref, edge_ref, products_in, gram_in, traces_ref, products_ref, gram_ref):
    z, l, quad, core = position()
    products, gram = partial_products(1 - core, row_slice(quad), movie_ref, band_ref, edge_ref)
    plane_at = pl.multiple_of((1 - l) * 128, 128)
    edge_at = pl.multiple_of(l * 256, 128)
    products_ref[:, pl.ds(plane_at, 256)] = products[:, :256] + products_in[:, :256]
    products_ref[:, pl.ds(edge_at, 128)] = products[:, 256:] + products_in[:, 256:]
    for at, rows in ((plane_at, slice(0, 256)), (edge_at, slice(256, 384))):
        gram_ref[pl.ds(at, rows.stop - rows.start), pl.ds(plane_at, 256)] = gram[rows, :256] + gram_in[rows, :256]
        gram_ref[pl.ds(at, rows.stop - rows.start), pl.ds(edge_at, 128)] = gram[rows, 256:] + gram_in[rows, 256:]
    for half in range(2):
        traces_ref[half * 64:half * 64 + 64, :] = band_ref[core, half, quad, :, pl.ds(pl.multiple_of(l * 128, 128), 128)]


def body(planes, frames_data, footprints, traces, counts):
    rows, voxels = frames_data.shape
    share = voxels // 16
    half = rows // 2
    hbm = pl.BlockSpec(memory_space=pl.ANY)
    dma = pltpu.SemaphoreType.DMA
    chunks = voxels // CHUNK
    gathered = pl.pallas_call(
        functools.partial(exchange_kernel, planes),
        name="exchange",
        out_shape=[
            jax.ShapeDtypeStruct((2, 2, 8, half, share), BF16),
            jax.ShapeDtypeStruct((2, 2, 8, half, 256), BF16),
            jax.ShapeDtypeStruct((2, 2, 8, half, 128), BF16),
            jax.ShapeDtypeStruct((share, 384), F32),
            jax.ShapeDtypeStruct((384, 384), F32),
        ],
        in_specs=[hbm, hbm, hbm, hbm],
        out_specs=[pl.BlockSpec(memory_space=pltpu.VMEM)] * 5,
        scratch_shapes=[
            pltpu.SMEM((counts.shape[0],), jnp.int32),
            pltpu.VMEM((voxels, 384), BF16), pltpu.VMEM((400 + rows, voxels), BF16), pltpu.VMEM((6, rows, 128), BF16),
            pltpu.VMEM((400 + rows, 384), F32),
            pltpu.VMEM((2, half + 8, 256), F32), pltpu.VMEM((2, half + 8, 128), F32),
            pltpu.VMEM((half + 8, 256), F32), pltpu.VMEM((2, half + 8, 128), F32),
            pltpu.VMEM((2, 384, 256), BF16), pltpu.VMEM((384, 128), BF16), pltpu.VMEM((2, 384, 128), BF16),
            pltpu.VMEM((768, 256), BF16),
            pltpu.VMEM((ITERS, 3, half, 256), BF16), pltpu.VMEM((half, 256), BF16), pltpu.VMEM((2, half, 128), BF16),
            dma((chunks, 4)), dma((16,)), dma((16,)), dma((5,)), dma((6,)), dma((3,)), dma((3,)),
            dma((3,)), dma((3,)), dma((ITERS, 2)), dma((ITERS, 2)), dma((16,)), dma((16,)),
            dma((2, 8)), dma((2, 8)), dma((11,)), dma((11,)), dma((4,)), pltpu.SemaphoreType.REGULAR,
        ],
        compiler_params=pltpu.CompilerParams(collective_id=0, has_side_effects=True, vmem_limit_bytes=32 << 20),
    )(*[pltpu.with_memory_space_constraint(v, pltpu.HBM) for v in (counts, frames_data.reshape(2, half, voxels), footprints, traces)])
    vmem = pl.BlockSpec(memory_space=pltpu.VMEM)
    return pl.pallas_call(
        product_kernel,
        name="products",
        out_shape=[
            jax.ShapeDtypeStruct((rows, 128), BF16),
            jax.ShapeDtypeStruct((share, 384), F32),
            jax.ShapeDtypeStruct((384, 384), F32),
        ],
        in_specs=[vmem] * 5,
        out_specs=[vmem] * 3,
        compiler_params=pltpu.CompilerParams(vmem_limit_bytes=32 << 20),
    )(*gathered)


def solution(mesh):
    return jax.shard_map(
        functools.partial(body, mesh.shape["vox"] // 2),
        mesh=mesh,
        in_specs=(P("tm", "vox"), P("vox", None), P("tm", "vox"), P()),
        out_specs=(P("tm", "vox"), P(("vox", "tm"), None), P("vox", None)),
        check_vma=False,
    )
```

```python
import functools

import jax
import jax.numpy as jnp
from jax import lax
from jax.experimental import pallas as pl
from jax.experimental.pallas import tpu as pltpu
from jax.sharding import PartitionSpec as P

ITERS = 4
CHUNK = 1024
MESH = pl.DeviceIdType.MESH
F32 = jnp.float32
BF16 = jnp.bfloat16


def position():
    vox, tm = lax.axis_index("vox"), lax.axis_index("tm")
    return vox // 2, vox % 2, tm // 2, tm % 2


def turned(quad, dy, dx):
    return ((quad // 4 + dy) % 2) * 4 + (quad % 4 + dx) % 4


def exchange_kernel(
    planes,
    counts_hbm, frames_ref, prints_ref, traces_ref,
    movie_ref, band_ref, edge_ref, products_ref, gram_ref,
    counts_ref, prints, lefts, tracebuf, sums,
    part_plane, part_edge, got_plane, got_edge,
    gram_plane, gram_edge, got_gram, mixing,
    state, final, final_edge,
    load_sem, movie_send, movie_recv, trace_send, trace_recv, part_send, part_recv,
    gram_send, gram_recv, state_send, state_recv, band_send, band_recv,
    edge_send, edge_recv, pass_send, pass_recv, own_sem, met,
):
    z, l, quad, core = position()
    other = 1 - l
    up, down = (z + 1) % planes, (z + planes - 1) % planes
    outward = (z + planes - 1 + 2 * l) % planes
    below, above = z > 0, z < planes - 1
    beside = jnp.where(l == 0, z, planes - 1 - z) > 0
    always = None

    def given(condition, act):
        if condition is None:
            act()
        else:
            pl.when(condition)(act)

    def device(plane, side, q, c):
        return (plane * 2 + side, q * 2 + c)

    me = device(z, l, quad, core)
    across = turned(quad, 1, 0)
    offsets = [(dy, dx) for dy in range(2) for dx in range(4)]
    ring = [(dx, dc) for dx in (1, 3, 2, 0) for dc in range(2) if (dx, dc) != (0, 0)]
    barrier = pltpu.get_barrier_semaphore()
    near = [(always, device(z, other, quad, core))]
    near += [(there, device(plane, side, quad, core)) for there, plane in ((above, up), (below, down)) for side in range(2)]
    near += [(always, device(z, l, across, core))]
    near += [(always, device(z, l, turned(quad, 0, dx), (core + dc) % 2)) for dx, dc in ring]

    rows = prints_ref.shape[0]
    chunks = rows // CHUNK
    plane_at = pl.multiple_of((1 - l) * 128, 128)
    edge_at = pl.multiple_of(l * 256, 128)

    def loads(k):
        at = pl.multiple_of(k * CHUNK, CHUNK)
        return (
            pltpu.make_async_copy(prints_ref.at[pl.ds(at, CHUNK), pl.ds(plane_at, 256)], prints.at[pl.ds(at, CHUNK), pl.ds(0, 256)], load_sem.at[k, 0]),
            pltpu.make_async_copy(prints_ref.at[pl.ds(at, CHUNK), pl.ds(edge_at, 128)], prints.at[pl.ds(at, CHUNK), pl.ds(256, 128)], load_sem.at[k, 1]),
            pltpu.make_async_copy(frames_ref.at[0, :, pl.ds(at, CHUNK)], lefts.at[128:192, pl.ds(at, CHUNK)], load_sem.at[k, 2]),
            pltpu.make_async_copy(frames_ref.at[1, :, pl.ds(at, CHUNK)], lefts.at[192:256, pl.ds(at, CHUNK)], load_sem.at[k, 3]),
        )

    own_counts = pltpu.make_async_copy(counts_hbm, counts_ref, own_sem.at[3])
    own_counts.start()
    for k in range(chunks):
        for copy in loads(k):
            copy.start()
    own_trace = pltpu.make_async_copy(traces_ref, tracebuf.at[2 + l], own_sem.at[0])
    own_trace.start()
    share = movie_ref.shape[4]
    own_movie = pltpu.make_async_copy(
        frames_ref.at[:, :, pl.ds(pl.multiple_of((quad * 2 + core) * share, share), share)],
        movie_ref.at[core, :, quad], own_sem.at[1])
    own_movie.start()
    for there, target in near:
        given(there, functools.partial(pl.semaphore_signal, barrier, inc=1, device_id=target, device_id_type=MESH))

    @pl.when(jnp.logical_not(below))
    def _():
        tracebuf[0:2] = jnp.zeros((2,) + tracebuf.shape[1:], BF16)
        for step in range(1, ITERS):
            state[step, 0] = jnp.zeros(state.shape[2:], BF16)

    @pl.when(jnp.logical_not(above))
    def _():
        tracebuf[4:6] = jnp.zeros((2,) + tracebuf.shape[1:], BF16)
        for step in range(1, ITERS):
            state[step, 2] = jnp.zeros(state.shape[2:], BF16)

    @pl.when(jnp.logical_not(beside))
    def _():
        edge_ref[...] = jnp.zeros_like(edge_ref)

    own_counts.wait()

    def number(tile):
        inside = jnp.logical_and(tile >= 0, tile < 2 * planes)
        return jnp.where(inside, counts_ref[jnp.clip(tile, 0, 2 * planes - 1)], 0)

    numbers = [number(2 * z - 2 + s) for s in range(6)]
    edge_number = jnp.where(l == 0, numbers[1], numbers[4])
    lane = lax.broadcasted_iota(jnp.int32, (1, 128), 1)
    row = lax.broadcasted_iota(jnp.int32, (128, 1), 0)
    live_rows = jnp.concatenate(
        [(row < n).astype(F32) for n in (numbers[2], numbers[3], edge_number)], axis=0)
    live_lanes = [(lane < n).astype(F32) for n in numbers]
    own_live = jnp.concatenate([live_lanes[2], live_lanes[3]], axis=1)

    def turn(k):
        for copy in loads(k):
            copy.wait()
        at = pl.multiple_of(k * CHUNK, CHUNK)
        flipped = prints[pl.ds(at, CHUNK), :].T
        support = jnp.sum(flipped.astype(F32) * live_rows, axis=0, keepdims=True).astype(BF16)
        lefts[0:128, pl.ds(at, CHUNK)] = flipped[256:384]
        lefts[256:272, pl.ds(at, CHUNK)] = jnp.broadcast_to(support, (16, CHUNK))
        lefts[272:528, pl.ds(at, CHUNK)] = flipped[0:256]

    turn(0)
    pl.semaphore_wait(barrier, len(near) - 4 + 2 * below.astype(jnp.int32) + 2 * above.astype(jnp.int32))
    pl.semaphore_signal(met, inc=1, device_id=device(z, l, across, core), device_id_type=MESH)

    def to(src, dst, send, recv, plane, side, q=None):
        return pltpu.make_async_remote_copy(
            src, dst, send, recv, device_id=device(plane, side, quad if q is None else q, core), device_id_type=MESH)

    sent = []

    def send(there, copy):
        given(there, copy.start)
        sent.append((there, copy))

    send(always, to(traces_ref, tracebuf.at[2 + l], trace_send.at[0], trace_recv.at[2 + l], z, other))
    send(beside, to(traces_ref, tracebuf.at[4 - 3 * l], trace_send.at[1], trace_recv.at[4 - 3 * l], outward, other))

    inward = (z + planes + 1 - 2 * l) % planes
    half_rows = [pl.ds(pl.multiple_of(side * 64, 64), 64) for side in (l, other)]

    def trace_rows(k, plane, side, slot, part):
        return to(
            traces_ref.at[part], tracebuf.at[slot, part], trace_send.at[k], trace_recv.at[slot], plane, side)

    def movie_copy(dy, dx, dc):
        q, c = turned(quad, dy, dx), (core + dc) % 2
        slot = (dy * 4 + dx) * 2 + dc
        return pltpu.make_async_remote_copy(
            frames_ref.at[:, :, pl.ds(pl.multiple_of((q * 2 + c) * share, share), share)],
            movie_ref.at[core, :, quad], movie_send.at[slot], movie_recv.at[slot],
            device_id=device(z, l, q, c), device_id_type=MESH)

    for k in range(1, chunks):
        turn(k)
    sums[0:272, 256:384] = jnp.dot(lefts[0:272], prints[:, 256:384], preferred_element_type=F32)
    sums[:, 0:256] = jnp.dot(lefts[...], prints[:, 0:256], preferred_element_type=F32)

    sums[272:528, 256:384] = sums[0:128, 0:256].T
    gram = jnp.concatenate([sums[272:528, :], sums[0:128, :]], axis=0)
    high = gram.astype(BF16)
    low = (gram - high.astype(F32)).astype(BF16)
    gram_plane[l] = high[:, :256]
    gram_edge[...] = high[:, 256:]

    own_trace.wait()
    for there, slot in ((always, 2 + other), (beside, 1 + 3 * l)):
        given(there, to(traces_ref, tracebuf.at[slot], trace_send.at[0], trace_recv.at[slot], z, other).wait_recv)

    def trace(slot, live):
        return (tracebuf[slot].astype(F32) * live).astype(BF16)

    edge_live = jnp.where(l == 0, live_lanes[1], live_lanes[4])
    band = jnp.concatenate(
        [trace(2, live_lanes[2]), trace(3, live_lanes[3]), trace(1 + 3 * l, edge_live)], axis=1)
    reach = sums[256:264, :]
    parts = sums[128:256, :] - jnp.dot(
        jnp.concatenate([band, band], axis=1), jnp.concatenate([high, low], axis=0), preferred_element_type=F32)
    for half in range(2):
        piece = jnp.concatenate([parts[half * 64:half * 64 + 64], reach], axis=0)
        part_plane[half] = piece[:, :256]
        part_edge[half] = piece[:, 256:]
    pl.semaphore_wait(met, 1)

    send(always, to(part_plane.at[other], got_plane, part_send.at[0], part_recv.at[2], z, other))
    send(beside, to(part_edge.at[other], got_edge.at[other], part_send.at[2], part_recv.at[other], outward, other))
    send(beside, to(part_edge.at[l], got_edge.at[other], part_send.at[1], part_recv.at[other], outward, l))
    own_rows = pl.ds(pl.multiple_of(core * 192, 64), 192)
    send(always, to(gram_plane.at[l, own_rows], gram_plane.at[l, own_rows], gram_send.at[0], gram_recv.at[2], z, other, across))
    send(beside, to(gram_edge.at[own_rows], got_gram.at[other, own_rows], gram_send.at[2], gram_recv.at[other], outward, other, across))
    send(beside, to(gram_edge.at[own_rows], got_gram.at[other, own_rows], gram_send.at[1], gram_recv.at[other], outward, l))
    movie_copies = [movie_copy(0, dx, dc) for dx, dc in ring]
    for copy in movie_copies:
        copy.start()

    send(above, trace_rows(2, up, l, l, half_rows[0]))
    send(below, trace_rows(3, down, l, 4 + l, half_rows[0]))
    send(jnp.where(l == 0, z < planes - 1, z > 0), trace_rows(4, inward, other, 5 * l, half_rows[1]))
    to(part_plane.at[0], got_plane, part_send.at[0], part_recv.at[2], z, other).wait_recv()
    for there, slot in ((below, 0), (above, 1)):
        given(there, to(part_edge.at[0], got_edge.at[slot], part_send.at[0], part_recv.at[slot], z, other).wait_recv)
    total = part_plane[l] + got_plane[...] + jnp.concatenate(
        [jnp.where(below, got_edge[0], 0.0), jnp.where(above, got_edge[1], 0.0)], axis=1)
    slope = total[0:64]
    majorant = jnp.maximum(total[64:65], 1.0)

    def updated(current, slope):
        value = jnp.maximum(current.astype(F32) + slope / majorant, 0.0)
        return (value * own_live).astype(BF16)

    def send_state(step):
        send(above, to(state.at[step, 1], state.at[step, 0], state_send.at[step, 0], state_recv.at[step, 0], up, l))
        send(below, to(state.at[step, 1], state.at[step, 2], state_send.at[step, 1], state_recv.at[step, 1], down, l))

    mine = half_rows[0]

    def start_state(slots):
        for s in slots:
            value = (tracebuf[s, mine, :].astype(F32) * live_lanes[s]).astype(BF16)
            state[0, s // 2, :, (s % 2) * 128:(s % 2) * 128 + 128] = value

    start_state((2, 3))
    state[1, 1] = updated(state[0, 1], slope)
    send_state(1)

    late_movie = [movie_copy(1, dx, dc) for dc in range(2) for dx in (2, 1, 3, 0)]
    for copy in late_movie:
        copy.start()
    movie_copies += late_movie

    for there, slot in ((below, l), (above, 4 + l), (jnp.where(l == 0, z < planes - 1, z > 0), 5 - 5 * l)):
        given(there, trace_rows(2, z, other, slot, half_rows[0]).wait_recv)
    start_state((0, 1, 4, 5))

    sibling = (z * 2 + l, quad * 2 + 1 - core)

    def gram_pass(k, refs):
        ref = refs(own_rows)
        return pltpu.make_async_remote_copy(
            ref, ref, pass_send.at[k], pass_recv.at[k], device_id=sibling, device_id_type=MESH)

    gram_parts = [
        (always, 2, lambda part: gram_plane.at[other, part]),
        (below, 0, lambda part: got_gram.at[0, part]),
        (above, 1, lambda part: got_gram.at[1, part]),
    ]
    for there, k, refs in gram_parts:
        given(there, to(refs(own_rows), refs(own_rows), gram_send.at[0], gram_recv.at[k], z, other).wait_recv)
        send(there, gram_pass(k, refs))
    its_rows = pl.ds(pl.multiple_of((1 - core) * 192, 64), 192)
    for there, k, refs in gram_parts:
        given(there, pltpu.make_async_remote_copy(
            refs(its_rows), refs(its_rows), pass_send.at[k], pass_recv.at[k], device_id=sibling, device_id_type=MESH).wait_recv)
    ga, gb = gram_plane[0].astype(F32), gram_plane[1].astype(F32)
    gc = jnp.where(below, got_gram[0].astype(F32), 0.0)
    gd = jnp.where(above, got_gram[1].astype(F32), 0.0)
    mixing[0:128, 0:128] = gc[0:128].astype(BF16)
    mixing[0:128, 128:256] = jnp.zeros((128, 128), BF16)
    mixing[128:256, 0:128] = (gc[128:256] + ga[256:384, 0:128]).astype(BF16)
    mixing[128:256, 128:256] = ga[256:384, 128:256].astype(BF16)
    mixing[256:384, 0:128] = (gc[256:384] + ga[0:128, 0:128] + gb[0:128, 0:128]).astype(BF16)
    mixing[256:384, 128:256] = (ga[0:128, 128:256] + gb[0:128, 128:256]).astype(BF16)
    mixing[384:512, 0:128] = (ga[128:256, 0:128] + gb[128:256, 0:128]).astype(BF16)
    mixing[384:512, 128:256] = (ga[128:256, 128:256] + gb[128:256, 128:256] + gd[256:384]).astype(BF16)
    mixing[512:640, 0:128] = gb[256:384, 0:128].astype(BF16)
    mixing[512:640, 128:256] = (gb[256:384, 128:256] + gd[0:128]).astype(BF16)
    mixing[640:768, 0:128] = jnp.zeros((128, 128), BF16)
    mixing[640:768, 128:256] = gd[128:256].astype(BF16)

    def arrived(step):
        for there, side, slot in ((below, 0, 0), (above, 1, 2)):
            given(there, to(state.at[step, 1], state.at[step, slot], state_send.at[step, side], state_recv.at[step, side], z, other).wait_recv)

    base = slope
    for step in range(1, ITERS):
        first = 0 if step == 1 else step
        own = jnp.dot(
            jnp.concatenate([state[k, 1] for k in range(first, step + 1)], axis=0), mixing[256:512], preferred_element_type=F32)
        arrived(step)
        mix = own
        for slot in (0, 2):
            sides = jnp.concatenate([state[k, slot] for k in range(first, step + 1)], axis=0)
            mix = mix + jnp.dot(sides, mixing[slot * 256:slot * 256 + 256], preferred_element_type=F32)
        if step == 1:
            base = base + mix[:64]
            mix = mix[64:]
        value = updated(state[step, 1], base - mix)
        if step < ITERS - 1:
            state[step + 1, 1] = value
            send_state(step + 1)
        else:
            final[...] = value
            final_edge[0] = value[:, :128]
            final_edge[1] = value[:, 128:]

    def band_copy(dy, dx, dl):
        slot = (dy * 4 + dx) * 2 + dl
        return pltpu.make_async_remote_copy(
            final, band_ref.at[core, l, quad], band_send.at[slot], band_recv.at[slot],
            device_id=device(z, (l + dl) % 2, turned(quad, dy, dx), core), device_id_type=MESH)

    def edge_copy(dy, dx, side):
        slot = dy * 4 + dx
        return pltpu.make_async_remote_copy(
            final_edge.at[1 - side], edge_ref.at[core, l, quad], edge_send.at[side, slot], edge_recv.at[l, slot],
            device_id=device(up if side == 0 else down, side, turned(quad, dy, dx), core), device_id_type=MESH)

    own_band = pltpu.make_async_copy(final, band_ref.at[core, l, quad], own_sem.at[2])
    own_band.start()
    batches = [("edge", 1, 0), ("edge", 1, 1), ("band", 1, 0), ("band", 1, 1), ("edge", 0, 0), ("edge", 0, 1), ("band", 0, 1), ("band", 0, 0)]
    for kind, dy, side in batches:
        for dx in (2, 1, 3, 0):
            if kind == "edge":
                send(above if side == 0 else below, edge_copy(dy, dx, side))
            elif (dy, dx, side) != (0, 0, 0):
                send(always, band_copy(dy, dx, side))

    def row_of(kind, dy, side, c):
        yh = (quad // 4 + dy) % 2
        if kind == "edge":
            return edge_ref.at[c, side, pl.ds(yh * 4, 4)]
        return band_ref.at[c, (l + side) % 2, pl.ds(yh * 4, 4)]

    for k, (kind, dy, side) in enumerate(batches):
        there = beside if kind == "edge" else always
        for dx in range(4):
            slot = dy * 4 + dx
            if kind == "edge":
                given(there, pltpu.make_async_remote_copy(
                    final_edge.at[0], edge_ref.at[core, side, slot], edge_send.at[0, 0], edge_recv.at[side, slot],
                    device_id=sibling, device_id_type=MESH).wait_recv)
            elif (dy, dx, side) != (0, 0, 0):
                band_copy(dy, dx, side).wait_recv()
            else:
                own_band.wait()
        ref = row_of(kind, dy, side, core)
        send(there, pltpu.make_async_remote_copy(
            ref, ref, pass_send.at[3 + k], pass_recv.at[3 + k], device_id=sibling, device_id_type=MESH))

    def passed(k):
        kind, dy, side = batches[k]
        ref = row_of(kind, dy, side, 1 - core)
        given(beside if kind == "edge" else always, pltpu.make_async_remote_copy(
            ref, ref, pass_send.at[3 + k], pass_recv.at[3 + k], device_id=sibling, device_id_type=MESH).wait_recv)

    own_movie.wait()
    for copy in movie_copies:
        copy.wait_recv()
    every = slice(None)
    products_ref[...], gram_ref[...] = partial_products(core, every, movie_ref, band_ref, edge_ref)
    for k in range(4):
        passed(k)
    products, gram = partial_products(1 - core, row_slice(across), movie_ref, band_ref, edge_ref)
    products_ref[...] += products
    gram_ref[...] += gram
    for k in range(4, 8):
        passed(k)
    for there, copy in sent:
        given(there, copy.wait_send)
    for copy in movie_copies:
        copy.wait_send()


def row_slice(quad):
    return pl.ds(quad // 4 * 4, 4)


def partial_products(core, row, movie_ref, band_ref, edge_ref):
    def frames_of(ref):
        return ref[core, :, row].reshape(-1, ref.shape[-1])

    whole = jnp.concatenate([frames_of(band_ref), frames_of(edge_ref)], axis=1)

    def over_frames(left):
        return lax.dot_general(left, whole, (((0,), (0,)), ((), ())), preferred_element_type=F32)

    return over_frames(frames_of(movie_ref)), over_frames(whole)


def product_kernel(movie_ref, band_ref, edge_ref, products_in, gram_in, traces_ref, products_ref, gram_ref):
    z, l, quad, core = position()
    products, gram = partial_products(1 - core, row_slice(quad), movie_ref, band_ref, edge_ref)
    plane_at = pl.multiple_of((1 - l) * 128, 128)
    edge_at = pl.multiple_of(l * 256, 128)
    products_ref[:, pl.ds(plane_at, 256)] = products[:, :256] + products_in[:, :256]
    products_ref[:, pl.ds(edge_at, 128)] = products[:, 256:] + products_in[:, 256:]
    for at, rows in ((plane_at, slice(0, 256)), (edge_at, slice(256, 384))):
        gram_ref[pl.ds(at, rows.stop - rows.start), pl.ds(plane_at, 256)] = gram[rows, :256] + gram_in[rows, :256]
        gram_ref[pl.ds(at, rows.stop - rows.start), pl.ds(edge_at, 128)] = gram[rows, 256:] + gram_in[rows, 256:]
    for half in range(2):
        traces_ref[half * 64:half * 64 + 64, :] = band_ref[core, half, quad, :, pl.ds(pl.multiple_of(l * 128, 128), 128)]


def body(planes, frames_data, footprints, traces, counts):
    rows, voxels = frames_data.shape
    share = voxels // 16
    half = rows // 2
    hbm = pl.BlockSpec(memory_space=pl.ANY)
    dma = pltpu.SemaphoreType.DMA
    chunks = voxels // CHUNK
    gathered = pl.pallas_call(
        functools.partial(exchange_kernel, planes),
        name="exchange",
        out_shape=[
            jax.ShapeDtypeStruct((2, 2, 8, half, share), BF16),
            jax.ShapeDtypeStruct((2, 2, 8, half, 256), BF16),
            jax.ShapeDtypeStruct((2, 2, 8, half, 128), BF16),
            jax.ShapeDtypeStruct((share, 384), F32),
            jax.ShapeDtypeStruct((384, 384), F32),
        ],
        in_specs=[hbm, hbm, hbm, hbm],
        out_specs=[pl.BlockSpec(memory_space=pltpu.VMEM)] * 5,
        scratch_shapes=[
            pltpu.SMEM((counts.shape[0],), jnp.int32),
            pltpu.VMEM((voxels, 384), BF16), pltpu.VMEM((400 + rows, voxels), BF16), pltpu.VMEM((6, rows, 128), BF16),
            pltpu.VMEM((400 + rows, 384), F32),
            pltpu.VMEM((2, half + 8, 256), F32), pltpu.VMEM((2, half + 8, 128), F32),
            pltpu.VMEM((half + 8, 256), F32), pltpu.VMEM((2, half + 8, 128), F32),
            pltpu.VMEM((2, 384, 256), BF16), pltpu.VMEM((384, 128), BF16), pltpu.VMEM((2, 384, 128), BF16),
            pltpu.VMEM((768, 256), BF16),
            pltpu.VMEM((ITERS, 3, half, 256), BF16), pltpu.VMEM((half, 256), BF16), pltpu.VMEM((2, half, 128), BF16),
            dma((chunks, 4)), dma((16,)), dma((16,)), dma((5,)), dma((6,)), dma((3,)), dma((3,)),
            dma((3,)), dma((3,)), dma((ITERS, 2)), dma((ITERS, 2)), dma((16,)), dma((16,)),
            dma((2, 8)), dma((2, 8)), dma((11,)), dma((11,)), dma((4,)), pltpu.SemaphoreType.REGULAR,
        ],
        compiler_params=pltpu.CompilerParams(collective_id=0, has_side_effects=True, vmem_limit_bytes=32 << 20),
    )(*[pltpu.with_memory_space_constraint(v, pltpu.HBM) for v in (counts, frames_data.reshape(2, half, voxels), footprints, traces)])
    vmem = pl.BlockSpec(memory_space=pltpu.VMEM)
    return pl.pallas_call(
        product_kernel,
        name="products",
        out_shape=[
            jax.ShapeDtypeStruct((rows, 128), BF16),
            jax.ShapeDtypeStruct((share, 384), F32),
            jax.ShapeDtypeStruct((384, 384), F32),
        ],
        in_specs=[vmem] * 5,
        out_specs=[vmem] * 3,
        compiler_params=pltpu.CompilerParams(vmem_limit_bytes=32 << 20),
    )(*gathered)


def solution(mesh):
    return jax.shard_map(
        functools.partial(body, mesh.shape["vox"] // 2),
        mesh=mesh,
        in_specs=(P("tm", "vox"), P("vox", None), P("tm", "vox"), P()),
        out_specs=(P("tm", "vox"), P(("vox", "tm"), None), P("vox", None)),
        check_vma=False,
    )
```

```python
import functools

import jax
import jax.numpy as jnp
from jax import lax
from jax.experimental import pallas as pl
from jax.experimental.pallas import tpu as pltpu
from jax.sharding import PartitionSpec as P

ITERS = 4
CHUNK = 1024
MESH = pl.DeviceIdType.MESH
F32 = jnp.float32
BF16 = jnp.bfloat16


def position():
    vox, tm = lax.axis_index("vox"), lax.axis_index("tm")
    return vox // 2, vox % 2, tm // 2, tm % 2


def turned(quad, dy, dx):
    return ((quad // 4 + dy) % 2) * 4 + (quad % 4 + dx) % 4


def exchange_kernel(
    planes,
    counts_hbm, frames_ref, prints_ref, traces_ref,
    movie_ref, band_ref, edge_ref, products_ref, gram_ref,
    counts_ref, prints, lefts, tracebuf, sums,
    part_plane, part_edge, got_plane, got_edge,
    gram_plane, gram_edge, got_gram, mixing,
    state, final, final_edge,
    load_sem, movie_send, movie_recv, trace_send, trace_recv, part_send, part_recv,
    gram_send, gram_recv, state_send, state_recv, band_send, band_recv,
    edge_send, edge_recv, pass_send, pass_recv, own_sem, met,
):
    z, l, quad, core = position()
    other = 1 - l
    up, down = (z + 1) % planes, (z + planes - 1) % planes
    outward = (z + planes - 1 + 2 * l) % planes
    below, above = z > 0, z < planes - 1
    beside = jnp.where(l == 0, z, planes - 1 - z) > 0
    always = None

    def given(condition, act):
        if condition is None:
            act()
        else:
            pl.when(condition)(act)

    def device(plane, side, q, c):
        return (plane * 2 + side, q * 2 + c)

    me = device(z, l, quad, core)
    across = turned(quad, 1, 0)
    offsets = [(dy, dx) for dy in range(2) for dx in range(4)]
    ring = [(dx, dc) for dx in (1, 3, 2, 0) for dc in range(2) if (dx, dc) != (0, 0)]
    barrier = pltpu.get_barrier_semaphore()
    near = [(always, device(z, other, quad, core))]
    near += [(there, device(plane, side, quad, core)) for there, plane in ((above, up), (below, down)) for side in range(2)]
    near += [(always, device(z, l, across, core))]
    near += [(always, device(z, l, turned(quad, 0, dx), (core + dc) % 2)) for dx, dc in ring]

    rows = prints_ref.shape[0]
    chunks = rows // CHUNK
    plane_at = pl.multiple_of((1 - l) * 128, 128)
    edge_at = pl.multiple_of(l * 256, 128)

    def loads(k):
        at = pl.multiple_of(k * CHUNK, CHUNK)
        return (
            pltpu.make_async_copy(prints_ref.at[pl.ds(at, CHUNK), pl.ds(plane_at, 256)], prints.at[pl.ds(at, CHUNK), pl.ds(0, 256)], load_sem.at[k, 0]),
            pltpu.make_async_copy(prints_ref.at[pl.ds(at, CHUNK), pl.ds(edge_at, 128)], prints.at[pl.ds(at, CHUNK), pl.ds(256, 128)], load_sem.at[k, 1]),
            pltpu.make_async_copy(frames_ref.at[0, :, pl.ds(at, CHUNK)], lefts.at[128:192, pl.ds(at, CHUNK)], load_sem.at[k, 2]),
            pltpu.make_async_copy(frames_ref.at[1, :, pl.ds(at, CHUNK)], lefts.at[192:256, pl.ds(at, CHUNK)], load_sem.at[k, 3]),
        )

    own_counts = pltpu.make_async_copy(counts_hbm, counts_ref, own_sem.at[3])
    own_counts.start()
    for k in range(chunks):
        for copy in loads(k):
            copy.start()
    own_trace = pltpu.make_async_copy(traces_ref, tracebuf.at[2 + l], own_sem.at[0])
    own_trace.start()
    share = movie_ref.shape[4]
    own_movie = pltpu.make_async_copy(
        frames_ref.at[:, :, pl.ds(pl.multiple_of((quad * 2 + core) * share, share), share)],
        movie_ref.at[core, :, quad], own_sem.at[1])
    own_movie.start()
    for there, target in near:
        given(there, functools.partial(pl.semaphore_signal, barrier, inc=1, device_id=target, device_id_type=MESH))

    @pl.when(jnp.logical_not(below))
    def _():
        tracebuf[0:2] = jnp.zeros((2,) + tracebuf.shape[1:], BF16)
        for step in range(1, ITERS):
            state[step, 0] = jnp.zeros(state.shape[2:], BF16)

    @pl.when(jnp.logical_not(above))
    def _():
        tracebuf[4:6] = jnp.zeros((2,) + tracebuf.shape[1:], BF16)
        for step in range(1, ITERS):
            state[step, 2] = jnp.zeros(state.shape[2:], BF16)

    @pl.when(jnp.logical_not(beside))
    def _():
        edge_ref[...] = jnp.zeros_like(edge_ref)

    own_counts.wait()

    def number(tile):
        inside = jnp.logical_and(tile >= 0, tile < 2 * planes)
        return jnp.where(inside, counts_ref[jnp.clip(tile, 0, 2 * planes - 1)], 0)

    numbers = [number(2 * z - 2 + s) for s in range(6)]
    edge_number = jnp.where(l == 0, numbers[1], numbers[4])
    lane = lax.broadcasted_iota(jnp.int32, (1, 128), 1)
    row = lax.broadcasted_iota(jnp.int32, (128, 1), 0)
    live_rows = jnp.concatenate(
        [(row < n).astype(F32) for n in (numbers[2], numbers[3], edge_number)], axis=0)
    live_lanes = [(lane < n).astype(F32) for n in numbers]
    own_live = jnp.concatenate([live_lanes[2], live_lanes[3]], axis=1)

    def turn(k):
        for copy in loads(k):
            copy.wait()
        at = pl.multiple_of(k * CHUNK, CHUNK)
        flipped = prints[pl.ds(at, CHUNK), :].T
        support = jnp.sum(flipped.astype(F32) * live_rows, axis=0, keepdims=True).astype(BF16)
        lefts[0:128, pl.ds(at, CHUNK)] = flipped[256:384]
        lefts[256:272, pl.ds(at, CHUNK)] = jnp.broadcast_to(support, (16, CHUNK))
        lefts[272:528, pl.ds(at, CHUNK)] = flipped[0:256]

    turn(0)
    pl.semaphore_wait(barrier, len(near) - 4 + 2 * below.astype(jnp.int32) + 2 * above.astype(jnp.int32))
    pl.semaphore_signal(met, inc=1, device_id=device(z, l, across, core), device_id_type=MESH)

    def to(src, dst, send, recv, plane, side, q=None):
        return pltpu.make_async_remote_copy(
            src, dst, send, recv, device_id=device(plane, side, quad if q is None else q, core), device_id_type=MESH)

    sent = []

    def send(there, copy):
        given(there, copy.start)
        sent.append((there, copy))

    send(always, to(traces_ref, tracebuf.at[2 + l], trace_send.at[0], trace_recv.at[2 + l], z, other))
    send(beside, to(traces_ref, tracebuf.at[4 - 3 * l], trace_send.at[1], trace_recv.at[4 - 3 * l], outward, other))

    inward = (z + planes + 1 - 2 * l) % planes
    half_rows = [pl.ds(pl.multiple_of(side * 64, 64), 64) for side in (l, other)]

    def trace_rows(k, plane, side, slot, part):
        return to(
            traces_ref.at[part], tracebuf.at[slot, part], trace_send.at[k], trace_recv.at[slot], plane, side)

    def movie_copy(dy, dx, dc):
        q, c = turned(quad, dy, dx), (core + dc) % 2
        slot = (dy * 4 + dx) * 2 + dc
        return pltpu.make_async_remote_copy(
            frames_ref.at[:, :, pl.ds(pl.multiple_of((q * 2 + c) * share, share), share)],
            movie_ref.at[core, :, quad], movie_send.at[slot], movie_recv.at[slot],
            device_id=device(z, l, q, c), device_id_type=MESH)

    for k in range(1, chunks):
        turn(k)
    sums[0:272, 256:384] = jnp.dot(lefts[0:272], prints[:, 256:384], preferred_element_type=F32)
    sums[:, 0:256] = jnp.dot(lefts[...], prints[:, 0:256], preferred_element_type=F32)

    sums[272:528, 256:384] = sums[0:128, 0:256].T
    gram = jnp.concatenate([sums[272:528, :], sums[0:128, :]], axis=0)
    high = gram.astype(BF16)
    low = (gram - high.astype(F32)).astype(BF16)
    gram_plane[l] = high[:, :256]
    gram_edge[...] = high[:, 256:]

    pl.semaphore_wait(met, 1)
    own_rows = pl.ds(pl.multiple_of(core * 192, 64), 192)
    send(always, to(gram_plane.at[l, own_rows], gram_plane.at[l, own_rows], gram_send.at[0], gram_recv.at[2], z, other, across))
    send(beside, to(gram_edge.at[own_rows], got_gram.at[other, own_rows], gram_send.at[2], gram_recv.at[other], outward, other, across))
    send(beside, to(gram_edge.at[own_rows], got_gram.at[other, own_rows], gram_send.at[1], gram_recv.at[other], outward, l))

    own_trace.wait()
    for there, slot in ((always, 2 + other), (beside, 1 + 3 * l)):
        given(there, to(traces_ref, tracebuf.at[slot], trace_send.at[0], trace_recv.at[slot], z, other).wait_recv)

    def trace(slot, live):
        return (tracebuf[slot].astype(F32) * live).astype(BF16)

    edge_live = jnp.where(l == 0, live_lanes[1], live_lanes[4])
    band = jnp.concatenate(
        [trace(2, live_lanes[2]), trace(3, live_lanes[3]), trace(1 + 3 * l, edge_live)], axis=1)
    reach = sums[256:264, :]
    parts = sums[128:256, :] - jnp.dot(
        jnp.concatenate([band, band], axis=1), jnp.concatenate([high, low], axis=0), preferred_element_type=F32)
    for half in range(2):
        piece = jnp.concatenate([parts[half * 64:half * 64 + 64], reach], axis=0)
        part_plane[half] = piece[:, :256]
        part_edge[half] = piece[:, 256:]

    send(always, to(part_plane.at[other], got_plane, part_send.at[0], part_recv.at[2], z, other))
    send(beside, to(part_edge.at[other], got_edge.at[other], part_send.at[2], part_recv.at[other], outward, other))
    send(beside, to(part_edge.at[l], got_edge.at[other], part_send.at[1], part_recv.at[other], outward, l))
    movie_copies = [movie_copy(0, dx, dc) for dx, dc in ring]
    for copy in movie_copies:
        copy.start()

    send(above, trace_rows(2, up, l, l, half_rows[0]))
    send(below, trace_rows(3, down, l, 4 + l, half_rows[0]))
    send(jnp.where(l == 0, z < planes - 1, z > 0), trace_rows(4, inward, other, 5 * l, half_rows[1]))
    to(part_plane.at[0], got_plane, part_send.at[0], part_recv.at[2], z, other).wait_recv()
    for there, slot in ((below, 0), (above, 1)):
        given(there, to(part_edge.at[0], got_edge.at[slot], part_send.at[0], part_recv.at[slot], z, other).wait_recv)
    total = part_plane[l] + got_plane[...] + jnp.concatenate(
        [jnp.where(below, got_edge[0], 0.0), jnp.where(above, got_edge[1], 0.0)], axis=1)
    slope = total[0:64]
    majorant = jnp.maximum(total[64:65], 1.0)

    def updated(current, slope):
        value = jnp.maximum(current.astype(F32) + slope / majorant, 0.0)
        return (value * own_live).astype(BF16)

    def send_state(step):
        send(above, to(state.at[step, 1], state.at[step, 0], state_send.at[step, 0], state_recv.at[step, 0], up, l))
        send(below, to(state.at[step, 1], state.at[step, 2], state_send.at[step, 1], state_recv.at[step, 1], down, l))

    mine = half_rows[0]

    def start_state(slots):
        for s in slots:
            value = (tracebuf[s, mine, :].astype(F32) * live_lanes[s]).astype(BF16)
            state[0, s // 2, :, (s % 2) * 128:(s % 2) * 128 + 128] = value

    start_state((2, 3))
    state[1, 1] = updated(state[0, 1], slope)
    send_state(1)

    late_movie = [movie_copy(1, dx, dc) for dc in range(2) for dx in (2, 1, 3, 0)]
    for copy in late_movie:
        copy.start()
    movie_copies += late_movie

    for there, slot in ((below, l), (above, 4 + l), (jnp.where(l == 0, z < planes - 1, z > 0), 5 - 5 * l)):
        given(there, trace_rows(2, z, other, slot, half_rows[0]).wait_recv)
    start_state((0, 1, 4, 5))

    sibling = (z * 2 + l, quad * 2 + 1 - core)

    def gram_pass(k, refs):
        ref = refs(own_rows)
        return pltpu.make_async_remote_copy(
            ref, ref, pass_send.at[k], pass_recv.at[k], device_id=sibling, device_id_type=MESH)

    gram_parts = [
        (always, 2, lambda part: gram_plane.at[other, part]),
        (below, 0, lambda part: got_gram.at[0, part]),
        (above, 1, lambda part: got_gram.at[1, part]),
    ]
    for there, k, refs in gram_parts:
        given(there, to(refs(own_rows), refs(own_rows), gram_send.at[0], gram_recv.at[k], z, other).wait_recv)
        send(there, gram_pass(k, refs))
    its_rows = pl.ds(pl.multiple_of((1 - core) * 192, 64), 192)
    for there, k, refs in gram_parts:
        given(there, pltpu.make_async_remote_copy(
            refs(its_rows), refs(its_rows), pass_send.at[k], pass_recv.at[k], device_id=sibling, device_id_type=MESH).wait_recv)
    ga, gb = gram_plane[0].astype(F32), gram_plane[1].astype(F32)
    gc = jnp.where(below, got_gram[0].astype(F32), 0.0)
    gd = jnp.where(above, got_gram[1].astype(F32), 0.0)
    mixing[0:128, 0:128] = gc[0:128].astype(BF16)
    mixing[0:128, 128:256] = jnp.zeros((128, 128), BF16)
    mixing[128:256, 0:128] = (gc[128:256] + ga[256:384, 0:128]).astype(BF16)
    mixing[128:256, 128:256] = ga[256:384, 128:256].astype(BF16)
    mixing[256:384, 0:128] = (gc[256:384] + ga[0:128, 0:128] + gb[0:128, 0:128]).astype(BF16)
    mixing[256:384, 128:256] = (ga[0:128, 128:256] + gb[0:128, 128:256]).astype(BF16)
    mixing[384:512, 0:128] = (ga[128:256, 0:128] + gb[128:256, 0:128]).astype(BF16)
    mixing[384:512, 128:256] = (ga[128:256, 128:256] + gb[128:256, 128:256] + gd[256:384]).astype(BF16)
    mixing[512:640, 0:128] = gb[256:384, 0:128].astype(BF16)
    mixing[512:640, 128:256] = (gb[256:384, 128:256] + gd[0:128]).astype(BF16)
    mixing[640:768, 0:128] = jnp.zeros((128, 128), BF16)
    mixing[640:768, 128:256] = gd[128:256].astype(BF16)

    def arrived(step):
        for there, side, slot in ((below, 0, 0), (above, 1, 2)):
            given(there, to(state.at[step, 1], state.at[step, slot], state_send.at[step, side], state_recv.at[step, side], z, other).wait_recv)

    base = slope
    for step in range(1, ITERS):
        first = 0 if step == 1 else step
        own = jnp.dot(
            jnp.concatenate([state[k, 1] for k in range(first, step + 1)], axis=0), mixing[256:512], preferred_element_type=F32)
        arrived(step)
        mix = own
        for slot in (0, 2):
            sides = jnp.concatenate([state[k, slot] for k in range(first, step + 1)], axis=0)
            mix = mix + jnp.dot(sides, mixing[slot * 256:slot * 256 + 256], preferred_element_type=F32)
        if step == 1:
            base = base + mix[:64]
            mix = mix[64:]
        value = updated(state[step, 1], base - mix)
        if step < ITERS - 1:
            state[step + 1, 1] = value
            send_state(step + 1)
        else:
            final[...] = value
            final_edge[0] = value[:, :128]
            final_edge[1] = value[:, 128:]

    def band_copy(dy, dx, dl):
        slot = (dy * 4 + dx) * 2 + dl
        return pltpu.make_async_remote_copy(
            final, band_ref.at[core, l, quad], band_send.at[slot], band_recv.at[slot],
            device_id=device(z, (l + dl) % 2, turned(quad, dy, dx), core), device_id_type=MESH)

    def edge_copy(dy, dx, side):
        slot = dy * 4 + dx
        return pltpu.make_async_remote_copy(
            final_edge.at[1 - side], edge_ref.at[core, l, quad], edge_send.at[side, slot], edge_recv.at[l, slot],
            device_id=device(up if side == 0 else down, side, turned(quad, dy, dx), core), device_id_type=MESH)

    own_band = pltpu.make_async_copy(final, band_ref.at[core, l, quad], own_sem.at[2])
    own_band.start()
    batches = [("edge", 1, 0), ("edge", 1, 1), ("band", 1, 0), ("band", 1, 1), ("edge", 0, 0), ("edge", 0, 1), ("band", 0, 1), ("band", 0, 0)]
    for kind, dy, side in batches:
        for dx in (2, 1, 3, 0):
            if kind == "edge":
                send(above if side == 0 else below, edge_copy(dy, dx, side))
            elif (dy, dx, side) != (0, 0, 0):
                send(always, band_copy(dy, dx, side))

    def row_of(kind, dy, side, c):
        yh = (quad // 4 + dy) % 2
        if kind == "edge":
            return edge_ref.at[c, side, pl.ds(yh * 4, 4)]
        return band_ref.at[c, (l + side) % 2, pl.ds(yh * 4, 4)]

    for k, (kind, dy, side) in enumerate(batches):
        there = beside if kind == "edge" else always
        for dx in range(4):
            slot = dy * 4 + dx
            if kind == "edge":
                given(there, pltpu.make_async_remote_copy(
                    final_edge.at[0], edge_ref.at[core, side, slot], edge_send.at[0, 0], edge_recv.at[side, slot],
                    device_id=sibling, device_id_type=MESH).wait_recv)
            elif (dy, dx, side) != (0, 0, 0):
                band_copy(dy, dx, side).wait_recv()
            else:
                own_band.wait()
        ref = row_of(kind, dy, side, core)
        send(there, pltpu.make_async_remote_copy(
            ref, ref, pass_send.at[3 + k], pass_recv.at[3 + k], device_id=sibling, device_id_type=MESH))

    def passed(k):
        kind, dy, side = batches[k]
        ref = row_of(kind, dy, side, 1 - core)
        given(beside if kind == "edge" else always, pltpu.make_async_remote_copy(
            ref, ref, pass_send.at[3 + k], pass_recv.at[3 + k], device_id=sibling, device_id_type=MESH).wait_recv)

    own_movie.wait()
    for copy in movie_copies:
        copy.wait_recv()
    every = slice(None)
    products_ref[...], gram_ref[...] = partial_products(core, every, movie_ref, band_ref, edge_ref)
    for k in range(4):
        passed(k)
    products, gram = partial_products(1 - core, row_slice(across), movie_ref, band_ref, edge_ref)
    products_ref[...] += products
    gram_ref[...] += gram
    for k in range(4, 8):
        passed(k)
    for there, copy in sent:
        given(there, copy.wait_send)
    for copy in movie_copies:
        copy.wait_send()


def row_slice(quad):
    return pl.ds(quad // 4 * 4, 4)


def partial_products(core, row, movie_ref, band_ref, edge_ref):
    def frames_of(ref):
        return ref[core, :, row].reshape(-1, ref.shape[-1])

    whole = jnp.concatenate([frames_of(band_ref), frames_of(edge_ref)], axis=1)

    def over_frames(left):
        return lax.dot_general(left, whole, (((0,), (0,)), ((), ())), preferred_element_type=F32)

    return over_frames(frames_of(movie_ref)), over_frames(whole)


def product_kernel(movie_ref, band_ref, edge_ref, products_in, gram_in, traces_ref, products_ref, gram_ref):
    z, l, quad, core = position()
    products, gram = partial_products(1 - core, row_slice(quad), movie_ref, band_ref, edge_ref)
    plane_at = pl.multiple_of((1 - l) * 128, 128)
    edge_at = pl.multiple_of(l * 256, 128)
    products_ref[:, pl.ds(plane_at, 256)] = products[:, :256] + products_in[:, :256]
    products_ref[:, pl.ds(edge_at, 128)] = products[:, 256:] + products_in[:, 256:]
    for at, rows in ((plane_at, slice(0, 256)), (edge_at, slice(256, 384))):
        gram_ref[pl.ds(at, rows.stop - rows.start), pl.ds(plane_at, 256)] = gram[rows, :256] + gram_in[rows, :256]
        gram_ref[pl.ds(at, rows.stop - rows.start), pl.ds(edge_at, 128)] = gram[rows, 256:] + gram_in[rows, 256:]
    for half in range(2):
        traces_ref[half * 64:half * 64 + 64, :] = band_ref[core, half, quad, :, pl.ds(pl.multiple_of(l * 128, 128), 128)]


def body(planes, frames_data, footprints, traces, counts):
    rows, voxels = frames_data.shape
    share = voxels // 16
    half = rows // 2
    hbm = pl.BlockSpec(memory_space=pl.ANY)
    dma = pltpu.SemaphoreType.DMA
    chunks = voxels // CHUNK
    gathered = pl.pallas_call(
        functools.partial(exchange_kernel, planes),
        name="exchange",
        out_shape=[
            jax.ShapeDtypeStruct((2, 2, 8, half, share), BF16),
            jax.ShapeDtypeStruct((2, 2, 8, half, 256), BF16),
            jax.ShapeDtypeStruct((2, 2, 8, half, 128), BF16),
            jax.ShapeDtypeStruct((share, 384), F32),
            jax.ShapeDtypeStruct((384, 384), F32),
        ],
        in_specs=[hbm, hbm, hbm, hbm],
        out_specs=[pl.BlockSpec(memory_space=pltpu.VMEM)] * 5,
        scratch_shapes=[
            pltpu.SMEM((counts.shape[0],), jnp.int32),
            pltpu.VMEM((voxels, 384), BF16), pltpu.VMEM((400 + rows, voxels), BF16), pltpu.VMEM((6, rows, 128), BF16),
            pltpu.VMEM((400 + rows, 384), F32),
            pltpu.VMEM((2, half + 8, 256), F32), pltpu.VMEM((2, half + 8, 128), F32),
            pltpu.VMEM((half + 8, 256), F32), pltpu.VMEM((2, half + 8, 128), F32),
            pltpu.VMEM((2, 384, 256), BF16), pltpu.VMEM((384, 128), BF16), pltpu.VMEM((2, 384, 128), BF16),
            pltpu.VMEM((768, 256), BF16),
            pltpu.VMEM((ITERS, 3, half, 256), BF16), pltpu.VMEM((half, 256), BF16), pltpu.VMEM((2, half, 128), BF16),
            dma((chunks, 4)), dma((16,)), dma((16,)), dma((5,)), dma((6,)), dma((3,)), dma((3,)),
            dma((3,)), dma((3,)), dma((ITERS, 2)), dma((ITERS, 2)), dma((16,)), dma((16,)),
            dma((2, 8)), dma((2, 8)), dma((11,)), dma((11,)), dma((4,)), pltpu.SemaphoreType.REGULAR,
        ],
        compiler_params=pltpu.CompilerParams(collective_id=0, has_side_effects=True, vmem_limit_bytes=32 << 20),
    )(*[pltpu.with_memory_space_constraint(v, pltpu.HBM) for v in (counts, frames_data.reshape(2, half, voxels), footprints, traces)])
    vmem = pl.BlockSpec(memory_space=pltpu.VMEM)
    return pl.pallas_call(
        product_kernel,
        name="products",
        out_shape=[
            jax.ShapeDtypeStruct((rows, 128), BF16),
            jax.ShapeDtypeStruct((share, 384), F32),
            jax.ShapeDtypeStruct((384, 384), F32),
        ],
        in_specs=[vmem] * 5,
        out_specs=[vmem] * 3,
        compiler_params=pltpu.CompilerParams(vmem_limit_bytes=32 << 20),
    )(*gathered)


def solution(mesh):
    return jax.shard_map(
        functools.partial(body, mesh.shape["vox"] // 2),
        mesh=mesh,
        in_specs=(P("tm", "vox"), P("vox", None), P("tm", "vox"), P()),
        out_specs=(P("tm", "vox"), P(("vox", "tm"), None), P("vox", None)),
        check_vma=False,
    )
```
